256 devices in a mesh: dp: 16 (over y, z_hi), expert: 16 (over x, z_lo, core).
Axes of the slice: x: 4, y: 4, z: 8 (z_hi: 4, z_lo: 2; z = z_hi * 2 + z_lo), core: 2. Of those that a mesh axis runs over, the one named last changes fastest.
Arguments:
- tokens: bfloat16 [2048, 4096], P('expert'), may hold values from -6 to 6
- cotangent: bfloat16 [2048, 4096], P('expert', 'dp'), may hold values from -6 to 6
- routes: int32 [2048, 8], P('expert'), may hold values from 0 to 15, all different within a row; in each aligned block of 128 rows (0 to 127, 128 to 255, ...) at most 80 rows name the same one
- router_weight: float32 [2048, 8], P('expert'), may hold values from 0.03 to 0.5
- w_gate: bfloat16 [16, 4096, 2048], P('expert', None, 'dp'), may hold values from -0.09375 to 0.09375
- w_up: bfloat16 [16, 4096, 2048], P('expert', None, 'dp'), may hold values from -0.09375 to 0.09375
- w_down: bfloat16 [16, 2048, 4096], P('expert', None, 'dp'), may hold values from -0.125 to 0.125
- scale_gate: bfloat16 [16, 2048], P('expert', 'dp'), may hold values from 0.5 to 2
- scale_up: bfloat16 [16, 2048], P('expert', 'dp'), may hold values from 0.5 to 2
- scale_down: bfloat16 [16, 4096], P('expert', 'dp'), may hold values from 0.5 to 2
- swapped: int32 [16], replicated, may hold values from 0 to 1, as said below
Outputs:
- mixed: bfloat16 [2048, 4096], P('expert', 'dp')
- grad_gate: bfloat16 [16, 4096, 2048], P('expert', None, 'dp')
- grad_up: bfloat16 [16, 4096, 2048], P('expert', None, 'dp')
- grad_down: bfloat16 [16, 2048, 4096], P('expert', None, 'dp')
- grad_scale_in: bfloat16 [16, 2, 2048], P('expert', None, 'dp')
- grad_scale_out: bfloat16 [16, 4096], P('expert', 'dp')
The draws below stay inside these ranges and needn't reach their ends.
Inputs may be any that keep to these rules, and one draw needn't show every extreme that they name: `routes`: each row names 8 different experts; among the 128 rows of one device along expert no expert is named by more than 80 rows, a bound that some block reaches. swapped[j] equals swapped[(j + 8) mod 16]; both values occur.
All inputs are finite; a program needn't handle non-finite values.
Results may differ from the reference program's by a relative error of at most 0.0064.
Values may be sent and summed in bfloat16 or wider, within the bound.
A program may use at most 128 MiB of HBM per device.

```python
import math
import jax
import jax.numpy as jnp
import numpy as np
from jax import lax

D = 4096
FF = 2048
EXPERTS = 16
TOP = 8
TOK_DEV = 128
CAP = 80
TOKENS = 2048
N_EXPERT = 16


def draw_swapped(key, part):
    key = jax.random.fold_in(key, 7)
    lower = jax.random.randint(key, (EXPERTS // 2,), 0, 2)
    lower = lower.at[0].set(1 - lower[1])
    return jnp.concatenate([lower, lower]).astype(jnp.int32)


def levels(rng, shape, shards, low, largest):
    def one(dim, parts):
        draws = jax.random.uniform(jax.random.fold_in(jax.random.fold_in(rng, 6), dim), (parts,), jnp.float32, low / len(shards), largest / len(shards))
        return jnp.repeat(jnp.exp(draws), shape[dim] // parts).reshape((-1,) + (1,) * (len(shape) - dim - 1))

    loudness = one(*shards[0])
    for cut in shards[1:]:
        loudness = loudness * one(*cut)
    return loudness


def shared_out(key, own, number, rows, count, top, reach, skew):
    sequence = jax.random.permutation(key, count)
    packed, ordinary = shares(count, rows * top, reach, skew, True), shares(count, rows * top, reach, skew, False)
    places = jnp.arange(count)

    def named(sizes, turn):
        used = int((sizes > 0).sum())
        fixed = max(1, used // 4)
        shifted = fixed + (places - fixed + turn * (used - fixed)) % max(1, count - fixed)
        return jnp.zeros((count,), jnp.int32).at[sequence[jnp.where(places < fixed, places, shifted)]].set(jnp.asarray(sizes, jnp.int32))

    sizes = jnp.where(number % 4 == 0, named(packed, number // 4), named(ordinary, number - number // 4 - 1))
    mixed = jax.random.permutation(jax.random.fold_in(own, 3), count)
    donor, receiver = mixed[0:count // 2 * 2:2], mixed[1:count // 2 * 2:2]
    slack = jnp.minimum(sizes[donor] - 1, reach - sizes[receiver]) // 2
    slack = jnp.where((donor == sequence[0]) | (receiver == sequence[0]) | (sizes[receiver] == 0), 0, jnp.maximum(slack, 0))
    shifted = jax.random.randint(jax.random.fold_in(own, 4), (count // 2,), 0, 1 << 20) % (slack + 1)
    sizes = sizes.at[donor].add(-shifted).at[receiver].add(shifted)
    members = jnp.searchsorted(jnp.cumsum(sizes), jnp.arange(rows * top), side="right").astype(jnp.int32)
    grid = members.reshape(top, rows).T
    grid = grid[jax.random.permutation(jax.random.fold_in(own, 1), rows)]
    turn = jax.random.randint(jax.random.fold_in(own, 2), (rows, 1), 0, top)
    return jnp.take_along_axis(grid, (jnp.arange(top)[None, :] + turn) % top, axis=1)


def shares(count, total, reach, slope, full):
    loads = [(1 << 20) // math.isqrt(grade ** slope) + 1 for grade in range(1, count + 1)]
    largest = reach if full else min(reach, max(-(-total // count), total * loads[0] // sum(loads)))
    least = 1 if total - largest >= count - 1 else 0
    given, rest = [largest] + [least] * (count - 1), total - largest - least * (count - 1)
    while rest > 0:
        free = [i for i in range(1, count) if given[i] < largest] or [i for i in range(1, count) if given[i] < reach]
        mass, left = sum([loads[i] for i in free]), rest
        for i in free:
            addition = min(reach - given[i], max(1, left * loads[i] // mass), rest)
            given[i] = given[i] + addition
            rest = rest - addition
    return np.array(given)


def normal_values(key, shape, scale, reach, cuts=(), held_as=jnp.bfloat16):
    result = scale * jax.random.normal(key, shape, jnp.float32)
    if cuts:
        result = result * levels(key, shape, cuts, -0.22, 0.18)
    return jnp.clip(result, -reach, reach).astype(held_as)


def setup_inputs(seed: int = 0) -> dict:
    arg_keys = jax.random.split(jax.random.key(seed), 12)
    tokens = normal_values(arg_keys[0], (TOKENS, D), 1.0, 6.0, ((0, 16),))
    cotangent = normal_values(arg_keys[1], (TOKENS, D), 1.0, 6.0, ((0, 16), (1, 16)))
    routes_keys = jax.random.split(jax.random.fold_in(arg_keys[2], 1), TOKENS // TOK_DEV)
    routes_turns = jax.random.permutation(jax.random.fold_in(arg_keys[2], 3), TOKENS // TOK_DEV)
    routes = jax.vmap(lambda own, number: shared_out(jax.random.fold_in(arg_keys[2], 2), own, number, TOK_DEV, EXPERTS, TOP, CAP, 2))(routes_keys, routes_turns).reshape((TOKENS, TOP))
    router_weight = jnp.clip(jnp.exp(math.log(0.5) - 2.8134107 * jax.random.uniform(arg_keys[3], (TOKENS, TOP), jnp.float32) ** levels(arg_keys[3], (TOKENS, TOP), ((0, 16),), -0.2, 0.2)), 0.03, 0.5)
    w_gate = normal_values(arg_keys[4], (EXPERTS, D, FF), D ** -0.5, 0.09375, ((0, 16), (2, 16)))
    w_up = normal_values(arg_keys[5], (EXPERTS, D, FF), D ** -0.5, 0.09375, ((0, 16), (2, 16)))
    w_down = normal_values(arg_keys[6], (EXPERTS, FF, D), FF ** -0.5, 0.125, ((0, 16), (2, 16)))
    scale_gate = jnp.clip(jnp.exp(math.log(2.0) - 1.3862944 * jax.random.uniform(arg_keys[7], (EXPERTS, FF), jnp.float32) ** levels(arg_keys[7], (EXPERTS, FF), ((0, 16), (1, 16)), -0.2, 0.2)), 0.5, 2.0).astype(jnp.bfloat16)
    scale_up = jnp.clip(jnp.exp(math.log(2.0) - 1.3862944 * jax.random.uniform(arg_keys[8], (EXPERTS, FF), jnp.float32) ** levels(arg_keys[8], (EXPERTS, FF), ((0, 16), (1, 16)), -0.2, 0.2)), 0.5, 2.0).astype(jnp.bfloat16)
    scale_down = jnp.clip(jnp.exp(math.log(2.0) - 1.3862944 * jax.random.uniform(arg_keys[9], (EXPERTS, D), jnp.float32) ** levels(arg_keys[9], (EXPERTS, D), ((0, 16), (1, 16)), -0.2, 0.2)), 0.5, 2.0).astype(jnp.bfloat16)
    swapped = draw_swapped(jax.random.fold_in(arg_keys[11], 71), 0)
    return dict(tokens=tokens, cotangent=cotangent, routes=routes, router_weight=router_weight, w_gate=w_gate, w_up=w_up, w_down=w_down, scale_gate=scale_gate, scale_up=scale_up, scale_down=scale_down, swapped=swapped)


def reference(tokens, cotangent, routes, router_weight, w_gate, w_up, w_down, scale_gate, scale_up, scale_down, swapped):
    highest = lax.Precision.HIGHEST
    expert_ids = jnp.arange(EXPERTS, dtype=jnp.int32)
    combine = jnp.sum(jnp.where(routes[:, :, None] == expert_ids[None, None, :], router_weight[:, :, None], jnp.float32(0.0)), axis=1).astype(jnp.float32)
    tokens_f = tokens.astype(jnp.float32)
    grads_f = cotangent.astype(jnp.float32)
    rows_kept = N_EXPERT * CAP

    def per_expert(mixed_sum, index):
        chosen = jnp.sum((routes == index).astype(jnp.int32), axis=1).astype(jnp.int32)
        picked = jnp.argsort(1 - chosen, stable=True)[:rows_kept].astype(jnp.int32)
        weight_all = lax.dynamic_index_in_dim(combine, index, 1, keepdims=False)
        weight_col = jnp.take(weight_all, picked, axis=0)
        rows_x = jnp.take(tokens_f, picked, axis=0)
        rows_g = jnp.take(grads_f, picked, axis=0)
        gate_w = w_gate[index].astype(jnp.float32)
        up_w = w_up[index].astype(jnp.float32)
        down_w = w_down[index].astype(jnp.float32)
        gate_scale = scale_gate[index].astype(jnp.float32)
        up_scale = scale_up[index].astype(jnp.float32)
        down_scale = scale_down[index].astype(jnp.float32)
        routed_grad = (weight_col[:, None] * rows_g).astype(jnp.bfloat16)
        gate_pre = jnp.dot(rows_x, gate_w, precision=highest)
        up_pre = jnp.dot(rows_x, up_w, precision=highest)
        gate_act = gate_pre * gate_scale[None, :]
        up_act = up_pre * up_scale[None, :]
        sigmoid_gate = jax.nn.sigmoid(gate_act)
        silu_gate = gate_act * sigmoid_gate
        hidden = (silu_gate * up_act).astype(jnp.bfloat16)
        down_pre = jnp.dot(hidden.astype(jnp.float32), down_w, precision=highest)
        expert_out = (down_pre * down_scale[None, :]).astype(jnp.bfloat16)
        mixed_sum = mixed_sum.at[picked].add(weight_col[:, None] * expert_out.astype(jnp.float32))
        scale_out_grad = jnp.sum(routed_grad.astype(jnp.float32) * down_pre, axis=0)
        down_in = (routed_grad.astype(jnp.float32) * down_scale[None, :]).astype(jnp.bfloat16)
        down_in_f = down_in.astype(jnp.float32)
        down_weight_grad = jnp.dot(hidden.astype(jnp.float32).T, down_in_f, precision=highest)
        hidden_grad = jnp.dot(down_in_f, down_w.T, precision=highest)
        gate_grad = hidden_grad * up_act * sigmoid_gate * (1.0 + gate_act * (1.0 - sigmoid_gate))
        up_grad = hidden_grad * silu_gate
        scale_in_grad = jnp.stack([jnp.sum(gate_grad * gate_pre, axis=0), jnp.sum(up_grad * up_pre, axis=0)], axis=0)
        gate_in = (gate_grad * gate_scale[None, :]).astype(jnp.bfloat16).astype(jnp.float32)
        up_in = (up_grad * up_scale[None, :]).astype(jnp.bfloat16).astype(jnp.float32)
        gate_weight_grad = jnp.dot(rows_x.T, gate_in, precision=highest)
        up_weight_grad = jnp.dot(rows_x.T, up_in, precision=highest)
        results = (gate_weight_grad.astype(jnp.bfloat16), up_weight_grad.astype(jnp.bfloat16), down_weight_grad.astype(jnp.bfloat16), scale_in_grad.astype(jnp.bfloat16), scale_out_grad.astype(jnp.bfloat16))
        return mixed_sum, results

    mixed_total, stacked = lax.scan(per_expert, jnp.zeros((TOKENS, D), jnp.float32), expert_ids)
    slots = jnp.arange(EXPERTS, dtype=jnp.int32)
    partner = (slots + EXPERTS // 2) % EXPERTS
    order = jnp.where(swapped == 1, partner, slots).astype(jnp.int32)
    grad_gate = jnp.take(stacked[0], order, axis=0)
    grad_up = jnp.take(stacked[1], order, axis=0)
    grad_down = jnp.take(stacked[2], order, axis=0)
    grad_scale_in = jnp.take(stacked[3], order, axis=0)
    grad_scale_out = jnp.take(stacked[4], order, axis=0)
    return (mixed_total.astype(jnp.bfloat16), grad_gate, grad_up, grad_down, grad_scale_in, grad_scale_out)
```

```python
import jax
import jax.numpy as jnp
from jax import lax
from jax.experimental import pallas as pl
from jax.experimental.pallas import tpu as pltpu
from jax.sharding import PartitionSpec as P

MESH = pl.DeviceIdType.MESH
BF = jnp.bfloat16
F32 = jnp.float32
CAP = 80
BLK = 16
TOK = 128
D = 4096
ROWS = BLK * CAP
NCH = 4
CROWS = ROWS // NCH
TCH = 4
ZFIRST = (0,)
VMEM_LIMIT = 60 * 2**20
NT = (((1,), (1,)), ((), ()))
TN = (((0,), (0,)), ((), ()))


def place():
    dp = lax.axis_index("dp")
    ex = lax.axis_index("expert")
    y, zh = lax.div(dp, 4), lax.rem(dp, 4)
    x, zl, c = lax.div(ex, 4), lax.rem(lax.div(ex, 2), 2), lax.rem(ex, 2)
    return x, y, zh * 2 + zl, c


def device(x, y, z, c):
    x, y, z, c = lax.rem(x + 4, 4), lax.rem(y + 4, 4), lax.rem(z + 8, 8), lax.rem(c + 2, 2)
    return (y * 4 + lax.div(z, 2), slot(x, z, c))


def slot(x, z, c):
    return lax.rem(x + 4, 4) * 4 + lax.rem(z + 8, 2) * 2 + c


class Links:
    def __init__(self, send_sems, recv_sems, other):
        self.ss, self.rs, self.other = send_sems, recv_sems, other
        self.copies = []

    def send(self, src, dst, to):
        i = len(self.copies)
        copy = pltpu.make_async_remote_copy(
            src_ref=src,
            dst_ref=dst,
            send_sem=self.ss.at[i],
            recv_sem=self.rs.at[i],
            device_id=to,
            device_id_type=MESH,
        )
        copy.start()
        self.copies.append(copy)
        return i

    def arrived(self, i, dst):
        pltpu.make_async_remote_copy(
            src_ref=dst,
            dst_ref=dst,
            send_sem=self.ss.at[i],
            recv_sem=self.rs.at[i],
            device_id=self.other,
            device_id_type=MESH,
        ).wait_recv()

    def finish(self):
        for copy in self.copies:
            copy.wait_send()


def greet(devices):
    barrier = pltpu.get_barrier_semaphore()
    for to in devices:
        pl.semaphore_signal(barrier, inc=1, device_id=to, device_id_type=MESH)
    pl.semaphore_wait(barrier, len(devices))


def gather_kernel(
    comb, cot, tok, wd, sd,
    toks, rg, di4, wd4, hg, cw_own, cw_par,
    cots, combs, pos, part, rz, ss, rs, local,
):
    x, y, z, c = place()
    zl = lax.rem(z, 2)
    zh = lax.div(z, 2)
    me = slot(x, z, c)
    sibling = device(x, y, z, 1 - c)
    chip = x * 2 + zl
    links = Links(ss, rs, sibling)

    def chip_at(k):
        q = lax.rem(chip + k + 8, 8)
        qx, qz = lax.div(q, 2), lax.rem(q, 2)
        return qx, zh * 2 + qz

    peers = [sibling]
    for k in range(1, 8):
        qx, qz = chip_at(k)
        peers.append(device(qx, y, qz, c))
    far_z = z - 1 + 2 * zl
    peers.append(device(x, y, far_z, c))
    for d in range(1, 4):
        peers.append(device(x, y + d, z, c))
        peers.append(device(x, y, z + 2 * d, c))
    greet(peers)

    first = []
    for k in range(1, 8):
        to = peers[k]
        first.append((k, links.send(comb, combs.at[me], to), links.send(cot, cots.at[me], to)))
    over = [(0, links.send(comb, combs.at[me], sibling), links.send(cot, cots.at[me], sibling))]
    wd_ids = []
    for d in (1, 3, 2):
        to_y = lax.rem(y + d, 4)
        rows = pl.ds(pl.multiple_of(to_y * 512, 512), 512)
        wd_ids.append((d, links.send(wd.at[rows], wd4.at[y], device(x, y + d, z, c))))
    own_tok = pltpu.make_async_copy(tok, toks.at[me], local.at[0])
    own_tok.start()
    combs[me] = comb[...]
    cots[me] = cot[...]
    wd4[y] = wd[pl.ds(pl.multiple_of(y * 512, 512), 512), :]
    for k, ia, ib in first:
        qx, qz = chip_at(-k)
        s = slot(qx, qz, c)
        links.arrived(ia, combs.at[s])
        links.arrived(ib, cots.at[s])
        over.append((k, links.send(combs.at[s], combs.at[s], sibling), links.send(cots.at[s], cots.at[s], sibling)))

    rt = TOK // TCH
    half = rt // 2

    def rows_of(k):
        return pl.ds(k * rt, rt)

    def low(k):
        return pl.ds(k * rt, half)

    def high(k):
        return pl.ds(k * rt + half, half)

    pair = []
    pair.append((links.send(tok, toks.at[me], sibling), lambda: toks.at[slot(x, z, 1 - c)]))
    xs, zs = {}, {}
    up, down = device(x, y, z + 1, c), device(x, y, z - 1, c)
    for k in range(TCH):
        for d in (1, 3, 2):
            xs[k, d] = links.send(tok.at[rows_of(k)], toks.at[me, rows_of(k)], device(x + d, y, z, c))
        zs[k, 0] = (
            links.send(tok.at[low(k)], toks.at[me, low(k)], up),
            links.send(tok.at[high(k)], toks.at[me, high(k)], down),
        )

    def to_sibling(sx, sz, k):
        s = slot(sx, sz, c)
        other = slot(sx, sz, 1 - c)
        i = links.send(toks.at[s, rows_of(k)], toks.at[s, rows_of(k)], sibling)
        pair.append((i, lambda: toks.at[other, rows_of(k)]))

    def x_event(k):
        for d in (1, 3, 2):
            s = slot(x - d, z, c)
            links.arrived(xs[k, d], toks.at[s, rows_of(k)])
            if k not in ZFIRST:
                zs[k, d] = (
                    links.send(toks.at[s, low(k)], toks.at[s, low(k)], up),
                    links.send(toks.at[s, high(k)], toks.at[s, high(k)], down),
                )
            to_sibling(x - d, z, k)

    def z_arrive(k, d):
        s = slot(x - d, z + 1, c)
        links.arrived(zs[k, d][0], toks.at[s, low(k)])
        links.arrived(zs[k, d][1], toks.at[s, high(k)])
        to_sibling(x - d, z + 1, k)
        return s

    x2 = {}

    def z_event(k):
        if k in ZFIRST:
            s = z_arrive(k, 0)
            for d in (1, 3, 2):
                x2[k, d] = links.send(toks.at[s, rows_of(k)], toks.at[s, rows_of(k)], device(x + d, y, z, c))
        else:
            for d in (0, 1, 3, 2):
                z_arrive(k, d)

    def x2_event(k):
        for d in (1, 3, 2):
            s = slot(x - d, z + 1, c)
            links.arrived(x2[k, d], toks.at[s, rows_of(k)])
            to_sibling(x - d, z + 1, k)

    for k, ia, ib in over:
        qx, qz = chip_at(-k)
        s = slot(qx, qz, 1 - c)
        links.arrived(ia, combs.at[s])
        links.arrived(ib, cots.at[s])

    experts = lax.broadcasted_iota(jnp.int32, (BLK, BLK, TOK), 1)
    table = combs[...]
    cw = jnp.sum(jnp.where(experts == me, table, 0.0), axis=1)
    cw_own[...] = cw
    cw_par[...] = jnp.sum(jnp.where(experts == lax.rem(me + 8, 16), table, 0.0), axis=1)
    before = lax.broadcasted_iota(jnp.int32, (TOK, TOK), 0) < lax.broadcasted_iota(jnp.int32, (TOK, TOK), 1)
    pos[...] = jnp.dot((cw > 0).astype(BF), before.astype(F32).astype(BF), preferred_element_type=F32)
    spots = lax.broadcasted_iota(jnp.int32, (CAP, TOK), 0).astype(F32)
    scale = sd[...].astype(F32)

    def compact(r, _):
        weight = cw_own[pl.ds(r, 1), :]
        hit = (pos[pl.ds(r, 1), :] == spots) & (weight > 0)
        picked = jnp.dot(jnp.where(hit, 1.0, 0.0).astype(BF), cots[r], preferred_element_type=F32)
        w = jnp.sum(jnp.where(hit, weight, 0.0), axis=1, keepdims=True)
        routed = (picked * w).astype(BF)
        rows = pl.ds(pl.multiple_of(r * CAP, CAP), CAP)
        rg[rows, :] = routed
        di4[y, rows, :] = (routed.astype(F32) * scale).astype(BF)
        return 0

    ys = {}
    for i in range(NCH):
        lax.fori_loop(i * (BLK // NCH), (i + 1) * (BLK // NCH), compact, 0)
        rows = pl.ds(i * CROWS, CROWS)
        for d in (1, 3, 2):
            ys[i, d] = links.send(di4.at[y, rows], di4.at[y, rows], device(x, y + d, z, c))
    for d, i in wd_ids:
        links.arrived(i, wd4.at[lax.rem(y - d + 4, 4)])

    zr = {}

    def terms(i):
        rows = pl.ds(i * CROWS, CROWS)
        for d in (1, 3, 2):
            links.arrived(ys[i, d], di4.at[lax.rem(y - d + 4, 4), rows])
        acc = lax.dot_general(di4[0, rows, :], wd4[0], NT, preferred_element_type=F32)
        for j in range(1, 4):
            acc += lax.dot_general(di4[j, rows, :], wd4[j], NT, preferred_element_type=F32)
        acc = acc.astype(BF)
        for j in range(4):
            part[j, rows, :] = acc[:, j * 128:(j + 1) * 128]
        for d in (2, 1, 3):
            zr[i, d] = links.send(part.at[lax.rem(zh + d, 4), rows], rz.at[d - 1, rows], device(x, y, z + 2 * d, c))

    def gradient(i):
        rows = pl.ds(i * CROWS, CROWS)
        for d in (1, 2, 3):
            links.arrived(zr[i, d], rz.at[d - 1, rows])
        total = part[zh, rows, :].astype(F32)
        for d in (1, 2, 3):
            total += rz[d - 1, rows, :].astype(F32)
        hg[rows, :] = total

    for i in range(NCH):
        terms(i)
        if i in ZFIRST:
            z_event(i)
        x_event(i)
    for i in range(NCH):
        if i in ZFIRST:
            x2_event(i)
        else:
            z_event(i)
    for i in range(NCH):
        gradient(i)
    for i, where in pair:
        links.arrived(i, where())
    own_tok.wait()
    links.finish()


def gather(comb, cot, tok, wd, sd):
    n = 170
    vm = pl.BlockSpec(memory_space=pltpu.VMEM)
    hbm = pl.BlockSpec(memory_space=pl.ANY)
    return pl.pallas_call(
        gather_kernel,
        out_shape=(
            jax.ShapeDtypeStruct((BLK, TOK, D), BF),
            jax.ShapeDtypeStruct((ROWS, 256), BF),
            jax.ShapeDtypeStruct((4, ROWS, 256), BF),
            jax.ShapeDtypeStruct((4, 512, 256), BF),
            jax.ShapeDtypeStruct((ROWS, 128), F32),
            jax.ShapeDtypeStruct((BLK, TOK), F32),
            jax.ShapeDtypeStruct((BLK, TOK), F32),
        ),
        in_specs=[vm, vm, hbm, vm, vm],
        out_specs=(hbm, vm, vm, vm, vm, vm, vm),
        scratch_shapes=[
            pltpu.VMEM((BLK, TOK, 256), BF),
            pltpu.VMEM((BLK, BLK, TOK), F32),
            pltpu.VMEM((BLK, TOK), F32),
            pltpu.VMEM((4, ROWS, 128), BF),
            pltpu.VMEM((3, ROWS, 128), BF),
            pltpu.SemaphoreType.DMA((n,)),
            pltpu.SemaphoreType.DMA((n,)),
            pltpu.SemaphoreType.DMA((1,)),
        ],
        name="gather",
        compiler_params=pltpu.CompilerParams(collective_id=0, has_side_effects=True, vmem_limit_bytes=VMEM_LIMIT),
    )(comb, cot, tok, wd, sd)


def down_kernel(
    hid, gi, sc, comb, comb_t, rg, di4, wd4, sd,
    mixed, own_gd, far_gd, gi_far, sc_far, so_own, so_far,
    hz, op, ro, eo, ret, gd, so, ss, rs,
):
    x, y, z, c = place()
    zh = lax.div(z, 2)
    me = slot(x, z, c)
    far = device(x + 2, y, z, c)
    links = Links(ss, rs, far)
    peers = []
    for k in range(1, 16):
        e = lax.rem(me + k, 16)
        peers.append((lax.axis_index("dp"), e))
    for d in range(1, 4):
        peers.append(device(x, y + d, z, c))
        peers.append(device(x, y, z + 2 * d, c))
        peers.append(device(x + 2, y + d, z, c))
    greet(peers)

    columns = pl.ds(pl.multiple_of(zh * 128, 128), 128)
    zs = {}
    order = [lax.rem(x + 1 + i, 4) for i in range(NCH)]

    def chunk(i):
        return pl.ds(pl.multiple_of(order[i] * CROWS, CROWS), CROWS)

    for i in range(NCH):
        rows = chunk(i)
        for d in (2, 1, 3):
            zs[i, d] = links.send(hid.at[rows], hz.at[rows, columns], device(x, y, z + 2 * d, c))
    gi_id = links.send(gi, gi_far, far)
    sc_id = links.send(sc, sc_far, far)
    hz[:, columns] = hid[...]

    ys = {}

    def project(i):
        rows = chunk(i)
        for d in (1, 3, 2):
            from_z = lax.rem(zh - d + 4, 4)
            links.arrived(zs[i, d], hz.at[rows, pl.ds(pl.multiple_of(from_z * 128, 128), 128)])
        left = hz[rows, :]
        for d in (2, 1, 3, 0):
            j = lax.rem(y + d, 4)
            op[j, rows, :] = jnp.dot(left, wd4[j], preferred_element_type=F32).astype(BF)
            if d:
                ys[i, d] = links.send(op.at[j, rows], ro.at[d - 1, rows], device(x, y + d, z, c))

    scale = sd[...].astype(F32)
    so[...] = jnp.zeros_like(so)
    back = {}
    inner = lax.rem(me, 4)

    def give(i):
        rows = chunk(i)
        for d in (1, 3, 2):
            links.arrived(ys[i, d], ro.at[d - 1, rows])
        total = op[y, rows, :].astype(F32)
        for d in (1, 2, 3):
            total += ro[d - 1, rows, :].astype(F32)
        so[0:1, :] += jnp.sum(total * rg[rows, :].astype(F32), axis=0, keepdims=True)
        eo[rows, :] = (total * scale).astype(BF)
        for j in range(4):
            r = order[i] * 4 + lax.rem(inner + j, 4)
            block = pl.ds(pl.multiple_of(r * CAP, CAP), CAP)
            if i == NCH - 1 and j == 0:
                ret[me] = eo[block, :]
            else:
                back[i, j] = links.send(eo.at[block], ret.at[me], (lax.axis_index("dp"), r))

    project(0)
    for i in range(1, NCH):
        project(i)
        give(i - 1)
    gds = {}
    for d in (1, 2, 3, 0):
        j = lax.rem(y + d, 4)
        gd[j] = lax.dot_general(hz[...], di4[j], TN, preferred_element_type=F32).astype(BF)
        rows = pl.ds(pl.multiple_of(y * 512, 512), 512)
        gds["far", d] = links.send(gd.at[j], far_gd.at[rows], device(x + 2, y + d, z, c))
        if d:
            gds["own", d] = links.send(gd.at[j], own_gd.at[rows], device(x, y + d, z, c))
        else:
            own_gd[rows, :] = gd[j]
    give(NCH - 1)
    so_id = links.send(so, so_far, far)
    so_own[...] = so[...]

    for (i, j), k in back.items():
        links.arrived(k, ret.at[lax.rem(x + 3 - i, 4) * 4 + lax.rem(inner + 4 - j, 4)])
    before = lax.broadcasted_iota(jnp.int32, (TOK, TOK), 0) < lax.broadcasted_iota(jnp.int32, (TOK, TOK), 1)
    places = jnp.dot((comb[...] > 0).astype(BF), before.astype(F32).astype(BF), preferred_element_type=F32)
    spots = lax.broadcasted_iota(jnp.int32, (CAP, TOK), 0).astype(F32)
    total = jnp.zeros((TOK, 256), F32)
    for e in range(BLK):
        weight = comb[e:e + 1, :]
        hit = (places[e:e + 1, :] == spots) & (weight > 0)
        spread = jnp.where(hit, 1.0, 0.0).astype(BF)
        total += lax.dot_general(spread, ret[e], TN, preferred_element_type=F32) * comb_t[:, e:e + 1]
    mixed[...] = total.astype(BF)
    links.arrived(gi_id, gi_far)
    links.arrived(sc_id, sc_far)
    links.arrived(so_id, so_far)
    for d in (1, 2, 3, 0):
        from_y = lax.rem(y - d + 4, 4)
        rows = pl.ds(pl.multiple_of(from_y * 512, 512), 512)
        links.arrived(gds["far", d], far_gd.at[rows])
        if d:
            links.arrived(gds["own", d], own_gd.at[rows])
    links.finish()


def down(hid, gi, sc, comb, comb_t, rg, di4, wd4, sd):
    n = 80
    vm = pl.BlockSpec(memory_space=pltpu.VMEM)
    return pl.pallas_call(
        down_kernel,
        out_shape=(
            jax.ShapeDtypeStruct((TOK, 256), BF),
            jax.ShapeDtypeStruct((2048, 256), BF),
            jax.ShapeDtypeStruct((2048, 256), BF),
            jax.ShapeDtypeStruct((ROWS, 256), BF),
            jax.ShapeDtypeStruct((8, 128), F32),
            jax.ShapeDtypeStruct((8, 256), F32),
            jax.ShapeDtypeStruct((8, 256), F32),
        ),
        in_specs=[vm] * 9,
        out_specs=[vm] * 7,
        scratch_shapes=[
            pltpu.VMEM((ROWS, 512), BF),
            pltpu.VMEM((4, ROWS, 256), BF),
            pltpu.VMEM((3, ROWS, 256), BF),
            pltpu.VMEM((ROWS, 256), BF),
            pltpu.VMEM((BLK, CAP, 256), BF),
            pltpu.VMEM((4, 512, 256), BF),
            pltpu.VMEM((8, 256), F32),
            pltpu.SemaphoreType.DMA((n,)),
            pltpu.SemaphoreType.DMA((n,)),
        ],
        name="down",
        compiler_params=pltpu.CompilerParams(collective_id=1, has_side_effects=True, vmem_limit_bytes=VMEM_LIMIT),
    )(hid, gi, sc, comb, comb_t, rg, di4, wd4, sd)


def picks(cw):
    mask = cw > 0
    place_of = jnp.cumsum(mask.astype(jnp.int32), axis=1) - 1
    spots = jnp.arange(CAP, dtype=jnp.int32)
    return ((place_of[:, None, :] == spots[None, :, None]) & mask[:, None, :]).astype(BF)


def per_device(
    tokens, cotangent, routes, router_weight, w_gate, w_up, w_down,
    scale_gate, scale_up, scale_down, swapped,
):
    me = lax.axis_index("expert")
    ids = jnp.arange(BLK, dtype=jnp.int32)
    flag = jnp.sum(jnp.where(ids == me, swapped, 0)) == 1
    comb_t = jnp.sum(jnp.where(routes[:, :, None] == ids, router_weight[:, :, None], 0.0), axis=1)
    comb = comb_t.T
    toks, rg, di4, wd4, hg, cw_own, cw_par = gather(comb, cotangent, tokens, w_down[0], scale_down)
    rows_x = jnp.einsum("rct,rtd->rcd", picks(cw_own), toks, preferred_element_type=F32).astype(BF).reshape(ROWS, D)
    gate_pre = jnp.dot(rows_x, w_gate[0], preferred_element_type=F32)
    up_pre = jnp.dot(rows_x, w_up[0], preferred_element_type=F32)
    gate_scale = scale_gate.astype(F32)
    up_scale = scale_up.astype(F32)
    gate_act = gate_pre * gate_scale
    up_act = up_pre * up_scale
    sig = jax.nn.sigmoid(gate_act)
    silu = gate_act * sig
    hidden = (silu * up_act).astype(BF)
    gate_grad = hg * up_act * sig * (1.0 + gate_act * (1.0 - sig))
    up_grad = hg * silu
    sc = jnp.concatenate(
        [
            jnp.sum(gate_grad * gate_pre, axis=0, keepdims=True),
            jnp.sum(up_grad * up_pre, axis=0, keepdims=True),
            jnp.zeros((6, 128), F32),
        ]
    )
    gi = jnp.concatenate([(gate_grad * gate_scale).astype(BF), (up_grad * up_scale).astype(BF)], axis=1)
    mixed, gd_own, gd_far, gi_far, sc_far, so_own, so_far = down(
        hidden, gi, sc, comb, comb_t, rg, di4, wd4, scale_down
    )
    chosen = jnp.where(flag, gi_far, gi).reshape(BLK, CAP, 256)
    spread = jnp.einsum(
        "rct,rcf->rtf", picks(jnp.where(flag, cw_par, cw_own)), chosen, preferred_element_type=F32
    ).astype(BF)
    wgrad = lax.dot_general(toks.reshape(BLK * TOK, D), spread.reshape(BLK * TOK, 256), TN, preferred_element_type=F32).astype(BF)
    grad_down = jnp.where(flag, gd_far, gd_own)
    scale_in = jnp.where(flag, sc_far, sc)[0:2].astype(BF)
    scale_out = jnp.where(flag, so_far, so_own)[0:1].astype(BF)
    return mixed, wgrad[None, :, :128], wgrad[None, :, 128:], grad_down[None], scale_in[None], scale_out


def solution(mesh):
    in_specs = (
        P("expert", None),
        P("expert", "dp"),
        P("expert", None),
        P("expert", None),
        P("expert", None, "dp"),
        P("expert", None, "dp"),
        P("expert", None, "dp"),
        P("expert", "dp"),
        P("expert", "dp"),
        P("expert", "dp"),
        P(),
    )
    out_specs = (
        P("expert", "dp"),
        P("expert", None, "dp"),
        P("expert", None, "dp"),
        P("expert", None, "dp"),
        P("expert", None, "dp"),
        P("expert", "dp"),
    )
    return jax.shard_map(
        per_device, mesh=mesh, in_specs=in_specs, out_specs=out_specs, check_vma=False
    )
```

```python
import jax
import jax.numpy as jnp
from jax import lax
from jax.experimental import pallas as pl
from jax.experimental.pallas import tpu as pltpu
from jax.sharding import PartitionSpec as P

MESH = pl.DeviceIdType.MESH
BF = jnp.bfloat16
F32 = jnp.float32
CAP = 80
BLK = 16
TOK = 128
D = 4096
ROWS = BLK * CAP
CROWS = ROWS // 4
VMEM_LIMIT = 60 * 2**20
NT = (((1,), (1,)), ((), ()))
TN = (((0,), (0,)), ((), ()))


def place():
    dp = lax.axis_index("dp")
    ex = lax.axis_index("expert")
    y, zh = lax.div(dp, 4), lax.rem(dp, 4)
    x, zl, c = lax.div(ex, 4), lax.rem(lax.div(ex, 2), 2), lax.rem(ex, 2)
    return x, y, zh * 2 + zl, c


def device(x, y, z, c):
    x, y, z, c = lax.rem(x + 4, 4), lax.rem(y + 4, 4), lax.rem(z + 8, 8), lax.rem(c + 2, 2)
    return (y * 4 + lax.div(z, 2), slot(x, z, c))


def slot(x, z, c):
    return lax.rem(x + 4, 4) * 4 + lax.rem(z + 8, 2) * 2 + c


class Links:
    def __init__(self, send_sems, recv_sems, other):
        self.ss, self.rs, self.other = send_sems, recv_sems, other
        self.copies = []

    def send(self, src, dst, to):
        i = len(self.copies)
        copy = pltpu.make_async_remote_copy(
            src_ref=src,
            dst_ref=dst,
            send_sem=self.ss.at[i],
            recv_sem=self.rs.at[i],
            device_id=to,
            device_id_type=MESH,
        )
        copy.start()
        self.copies.append(copy)
        return i

    def arrived(self, i, dst):
        pltpu.make_async_remote_copy(
            src_ref=dst,
            dst_ref=dst,
            send_sem=self.ss.at[i],
            recv_sem=self.rs.at[i],
            device_id=self.other,
            device_id_type=MESH,
        ).wait_recv()

    def finish(self):
        for copy in self.copies:
            copy.wait_send()


def greet(devices):
    barrier = pltpu.get_barrier_semaphore()
    for to in devices:
        pl.semaphore_signal(barrier, inc=1, device_id=to, device_id_type=MESH)
    pl.semaphore_wait(barrier, len(devices))


def layer_kernel(
    comb, comb_t, cot, tok, wg, wu, wd, sg, su, sd, flag,
    mixed, grad_t, own_gd, far_gd, sc, sc_far, so, so_far,
    toks, w_in, cots, combs, cw_own, cw_par, pos, rg, di4, wd4, part, rz,
    pre, hid, hz, hz_t, op, ro, eo, ret, gd, gi, gi_far, spread_t, ss, rs, local,
):
    x, y, z, c = place()
    zl = lax.rem(z, 2)
    zh = lax.div(z, 2)
    me = slot(x, z, c)
    inner = lax.rem(me, 4)
    dp = lax.axis_index("dp")
    sibling = device(x, y, z, 1 - c)
    far = device(x + 2, y, z, c)
    up, down = device(x, y, z + 1, c), device(x, y, z - 1, c)
    chip = x * 2 + zl
    links = Links(ss, rs, sibling)

    def chip_at(k):
        q = lax.rem(chip + k + 8, 8)
        return lax.div(q, 2), zh * 2 + lax.rem(q, 2)

    def columns(j):
        return pl.ds(pl.multiple_of(j * 128, 128), 128)

    def quarter(j):
        return pl.ds(pl.multiple_of(j * 512, 512), 512)

    def chunk(j):
        return pl.ds(pl.multiple_of(j * CROWS, CROWS), CROWS)

    def block(r):
        return pl.ds(pl.multiple_of(r * CAP, CAP), CAP)

    loads = [
        pltpu.make_async_copy(tok, toks.at[me], local.at[0]),
        pltpu.make_async_copy(wg, w_in.at[:, pl.ds(0, 128)], local.at[1]),
        pltpu.make_async_copy(wu, w_in.at[:, pl.ds(128, 128)], local.at[2]),
    ]
    for load in loads:
        load.start()

    peers = [(dp, lax.rem(me + k, 16)) for k in range(1, 16)]
    peers.append(device(x, y, z - 1 + 2 * zl, c))
    for d in range(1, 4):
        peers.append(device(x, y + d, z, c))
        peers.append(device(x, y, z + 2 * d, c))
        peers.append(device(x + 2, y + d, z, c))
    greet(peers)

    first = []
    for k in range(1, 8):
        qx, qz = chip_at(k)
        to = device(qx, y, qz, c)
        first.append((k, links.send(comb, combs.at[me], to), links.send(cot, cots.at[me], to)))
    over = [(0, links.send(comb, combs.at[me], sibling), links.send(cot, cots.at[me], sibling))]
    wd_ids = []
    for d in (1, 3, 2):
        wd_ids.append((d, links.send(wd.at[quarter(lax.rem(y + d, 4))], wd4.at[y], device(x, y + d, z, c))))

    lower, upper = pl.ds(0, 64), pl.ds(64, 64)
    third, fourth = pl.ds(64, 32), pl.ds(96, 32)
    pair = {}

    def to_sibling(d, dz, rows):
        s = slot(x - d, z + dz, c)
        pair.setdefault((d, dz), []).append((links.send(toks.at[s, rows], toks.at[s, rows], sibling), rows))

    pair[0, 0] = [(links.send(tok, toks.at[me], sibling), pl.ds(0, TOK))]
    z_ids, x_ids = {}, {}
    z_ids[0] = (
        links.send(tok.at[lower], toks.at[me, lower], up),
        links.send(tok.at[upper], toks.at[me, upper], down),
    )
    for rows, name in ((upper, "u"), (lower, "l")):
        for d in (1, 3):
            x_ids[d, name] = links.send(tok.at[rows], toks.at[me, rows], device(x + d, y, z, c))

    combs[me] = comb[...]
    cots[me] = cot[...]
    wd4[y] = wd[quarter(y), :]
    for k, ia, ib in first:
        qx, qz = chip_at(-k)
        s = slot(qx, qz, c)
        links.arrived(ia, combs.at[s])
        links.arrived(ib, cots.at[s])
        over.append((k, links.send(combs.at[s], combs.at[s], sibling), links.send(cots.at[s], cots.at[s], sibling)))
    for k, ia, ib in over:
        qx, qz = chip_at(-k)
        s = slot(qx, qz, 1 - c)
        links.arrived(ia, combs.at[s])
        links.arrived(ib, cots.at[s])

    experts = lax.broadcasted_iota(jnp.int32, (BLK, BLK, TOK), 1)
    table = combs[...]
    cw = jnp.sum(jnp.where(experts == me, table, 0.0), axis=1)
    cw_own[...] = cw
    cw_par[...] = jnp.sum(jnp.where(experts == lax.rem(me + 8, 16), table, 0.0), axis=1)
    before = (
        lax.broadcasted_iota(jnp.int32, (TOK, TOK), 0) < lax.broadcasted_iota(jnp.int32, (TOK, TOK), 1)
    ).astype(F32).astype(BF)
    pos[...] = jnp.dot((cw > 0).astype(BF), before, preferred_element_type=F32)
    spots = lax.broadcasted_iota(jnp.int32, (CAP, TOK), 0).astype(F32)
    down_scale = sd[...].astype(F32)

    def compact(r, _):
        weight = cw_own[pl.ds(r, 1), :]
        hit = (pos[pl.ds(r, 1), :] == spots) & (weight > 0)
        picked = jnp.dot(jnp.where(hit, 1.0, 0.0).astype(BF), cots[r], preferred_element_type=F32)
        w = jnp.sum(jnp.where(hit, weight, 0.0), axis=1, keepdims=True)
        routed = (picked * w).astype(BF)
        rg[block(r), :] = routed
        di4[y, block(r), :] = (routed.astype(F32) * down_scale).astype(BF)
        return 0

    y_ids = {}
    for i in range(4):
        lax.fori_loop(i * 4, i * 4 + 4, compact, 0)
        rows = pl.ds(i * CROWS, CROWS)
        for d in (1, 3, 2):
            y_ids[i, d] = links.send(di4.at[y, rows], di4.at[y, rows], device(x, y + d, z, c))
    for d, i in wd_ids:
        links.arrived(i, wd4.at[lax.rem(y - d + 4, 4)])

    zr = {}

    def terms(i):
        rows = pl.ds(i * CROWS, CROWS)
        for d in (1, 3, 2):
            links.arrived(y_ids[i, d], di4.at[lax.rem(y - d + 4, 4), rows])
        acc = lax.dot_general(di4[0, rows, :], wd4[0], NT, preferred_element_type=F32)
        for j in range(1, 4):
            acc += lax.dot_general(di4[j, rows, :], wd4[j], NT, preferred_element_type=F32)
        acc = acc.astype(BF)
        for j in range(4):
            part[j, rows, :] = acc[:, j * 128:(j + 1) * 128]
        for d in (2, 1, 3):
            zr[i, d] = links.send(part.at[lax.rem(zh + d, 4), rows], rz.at[d - 1, rows], device(x, y, z + 2 * d, c))

    def z_own():
        s = slot(x, z + 1, c)
        links.arrived(z_ids[0][0], toks.at[s, lower])
        for d in (1, 3):
            x_ids[d, "z"] = links.send(toks.at[s, lower], toks.at[s, lower], device(x + d, y, z, c))
        to_sibling(0, 1, lower)
        links.arrived(z_ids[0][1], toks.at[s, upper])
        to_sibling(0, 1, upper)

    def x_near():
        for d in (1, 3):
            s = slot(x - d, z, c)
            links.arrived(x_ids[d, "u"], toks.at[s, upper])
            z_ids[d] = (
                links.send(toks.at[s, third], toks.at[s, third], up),
                links.send(toks.at[s, fourth], toks.at[s, fourth], down),
            )
            to_sibling(d, 0, upper)
        for rows, name in ((lower, "l"), (upper, "u")):
            x_ids[2, name] = links.send(tok.at[rows], toks.at[me, rows], far)
        for d in (1, 3):
            s = slot(x - d, z, c)
            links.arrived(x_ids[d, "l"], toks.at[s, lower])
            to_sibling(d, 0, lower)

    def near_rest():
        for d in (1, 3):
            s = slot(x - d, z + 1, c)
            links.arrived(x_ids[d, "z"], toks.at[s, lower])
            to_sibling(d, 1, lower)
        for d in (1, 3):
            s = slot(x - d, z + 1, c)
            links.arrived(z_ids[d][0], toks.at[s, third])
            links.arrived(z_ids[d][1], toks.at[s, fourth])
            to_sibling(d, 1, upper)

    def x_far():
        s = slot(x + 2, z, c)
        links.arrived(x_ids[2, "l"], toks.at[s, lower])
        a = links.send(toks.at[s, lower], toks.at[s, lower], up)
        to_sibling(2, 0, lower)
        links.arrived(x_ids[2, "u"], toks.at[s, upper])
        b = links.send(toks.at[s, upper], toks.at[s, upper], down)
        to_sibling(2, 0, upper)
        z_ids[2] = (a, b)

    def z_far():
        s = slot(x + 2, z + 1, c)
        links.arrived(z_ids[2][0], toks.at[s, lower])
        to_sibling(2, 1, lower)
        links.arrived(z_ids[2][1], toks.at[s, upper])
        to_sibling(2, 1, upper)

    gate_scale = sg[...].astype(F32)
    up_scale = su[...].astype(F32)
    hid_ids = {}

    def group(d):
        gx = lax.rem(x - d + 4, 4)
        for dz in (0, 1):
            s = slot(x - d, z + dz, 1 - c)
            for i, rows in pair[d, dz]:
                links.arrived(i, toks.at[s, rows])

        def deepen(k, acc):
            at = pl.ds(pl.multiple_of(k * 1024, 1024), 1024)
            left = toks[pl.ds(gx * 4, 4), :, at].reshape(4 * TOK, 1024)
            return acc + jnp.dot(left, w_in[at, :], preferred_element_type=F32)

        acc = lax.fori_loop(0, 4, deepen, jnp.zeros((4 * TOK, 256), F32))
        for j in range(4):
            r = gx * 4 + j
            hit = (pos[pl.ds(r, 1), :] == spots) & (cw_own[pl.ds(r, 1), :] > 0)
            pre[block(r), :] = jnp.dot(
                jnp.where(hit, 1.0, 0.0), acc[j * TOK:(j + 1) * TOK], precision=lax.Precision.HIGHEST,
                preferred_element_type=F32,
            )
        rows = chunk(gx)
        gate_act = pre[rows, 0:128] * gate_scale
        up_act = pre[rows, 128:256] * up_scale
        hid[rows, :] = (gate_act * jax.nn.sigmoid(gate_act) * up_act).astype(BF)
        hz[rows, columns(zh)] = hid[rows, :]
        for dz in (2, 1, 3):
            hid_ids[d, dz] = links.send(hid.at[rows], hz.at[rows, columns(zh)], device(x, y, z + 2 * dz, c))

    out_ids = {}

    def project(d):
        rows = chunk(lax.rem(x - d + 4, 4))
        for dz in (1, 3, 2):
            links.arrived(hid_ids[d, dz], hz.at[rows, columns(lax.rem(zh - dz + 4, 4))])
        left = hz[rows, :]
        for dy in (2, 1, 3, 0):
            j = lax.rem(y + dy, 4)
            op[j, rows, :] = jnp.dot(left, wd4[j], preferred_element_type=F32).astype(BF)
            if dy:
                out_ids[d, dy] = links.send(op.at[j, rows], ro.at[dy - 1, rows], device(x, y + dy, z, c))

    so[...] = jnp.zeros_like(so)
    back = {}

    def give(d):
        gx = lax.rem(x - d + 4, 4)
        rows = chunk(gx)
        for dy in (1, 3, 2):
            links.arrived(out_ids[d, dy], ro.at[dy - 1, rows])
        total = op[y, rows, :].astype(F32)
        for dy in (1, 2, 3):
            total += ro[dy - 1, rows, :].astype(F32)
        so[0:1, :] += jnp.sum(total * rg[rows, :].astype(F32), axis=0, keepdims=True)
        eo[rows, :] = (total * down_scale).astype(BF)
        for j in range(4):
            r = gx * 4 + lax.rem(inner + j, 4)
            if d == 0 and j == 0:
                ret[me] = eo[block(r), :]
            else:
                back[d, j] = links.send(eo.at[block(r)], ret.at[me], (dp, r))

    sc[...] = jnp.zeros_like(sc)
    gi_ids = {}

    def gradient(i):
        rows = pl.ds(i * CROWS, CROWS)
        for d in (1, 2, 3):
            links.arrived(zr[i, d], rz.at[d - 1, rows])
        total = part[zh, rows, :].astype(F32)
        for d in (1, 2, 3):
            total += rz[d - 1, rows, :].astype(F32)
        gate_pre, up_pre = pre[rows, 0:128], pre[rows, 128:256]
        gate_act, up_act = gate_pre * gate_scale, up_pre * up_scale
        sig = jax.nn.sigmoid(gate_act)
        gate_grad = total * up_act * sig * (1.0 + gate_act * (1.0 - sig))
        up_grad = total * (gate_act * sig)
        sc[0:1, :] += jnp.sum(gate_grad * gate_pre, axis=0, keepdims=True)
        sc[1:2, :] += jnp.sum(up_grad * up_pre, axis=0, keepdims=True)
        gi[rows, 0:128] = (gate_grad * gate_scale).astype(BF)
        gi[rows, 128:256] = (up_grad * up_scale).astype(BF)
        gi_ids[i] = links.send(gi.at[rows], gi_far.at[rows], far)

    for load in loads:
        load.wait()
    z_own()
    group(0)
    terms(0)
    x_near()
    terms(1)
    near_rest()
    terms(2)
    group(1)
    group(3)
    terms(3)
    x_far()
    project(0)
    z_far()
    group(2)
    project(1)
    give(0)
    for i in range(4):
        gradient(i)
    sc_id = links.send(sc, sc_far, far)
    project(3)
    give(1)
    project(2)

    hz_t[...] = hz[...].T
    gd_ids = {}
    for d in (2, 1, 3, 0):
        j = lax.rem(y + d, 4)
        gd[j] = jnp.dot(hz_t[...], di4[j], preferred_element_type=F32).astype(BF)
        gd_ids["far", d] = links.send(gd.at[j], far_gd.at[quarter(y)], device(x + 2, y + d, z, c))
        if d:
            gd_ids["own", d] = links.send(gd.at[j], own_gd.at[quarter(y)], device(x, y + d, z, c))
        else:
            own_gd[quarter(y), :] = gd[j]
    give(3)
    give(2)
    so_id = links.send(so, so_far, far)

    for i in range(4):
        links.arrived(gi_ids[i], gi_far.at[pl.ds(i * CROWS, CROWS)])
    trade = flag[...] > 0
    cw_sel = jnp.where(trade[:, 0:128], cw_par[...], cw_own[...])
    cw_par[...] = cw_sel
    pos[...] = jnp.dot((cw_sel > 0).astype(BF), before, preferred_element_type=F32)

    def expand(r, _):
        hit = (pos[pl.ds(r, 1), :] == spots) & (cw_par[pl.ds(r, 1), :] > 0)
        chosen = jnp.where(trade, gi_far[block(r), :].astype(F32), gi[block(r), :].astype(F32)).astype(BF)
        spread_t[:, columns(r)] = lax.dot_general(
            chosen, jnp.where(hit, 1.0, 0.0).astype(BF), TN, preferred_element_type=F32
        ).astype(BF)
        return 0

    lax.fori_loop(0, BLK, expand, 0)

    def weight_grad(k, _):
        at = pl.ds(pl.multiple_of(k * 512, 512), 512)
        right = toks[:, :, at].reshape(BLK * TOK, 512)
        grad_t[:, at] = jnp.dot(spread_t[...], right, preferred_element_type=F32).astype(BF)
        return 0

    lax.fori_loop(0, D // 512, weight_grad, 0)

    for (d, j), k in back.items():
        links.arrived(k, ret.at[lax.rem(x + d, 4) * 4 + lax.rem(inner + 4 - j, 4)])
    places = jnp.dot((comb[...] > 0).astype(BF), before, preferred_element_type=F32)
    total = jnp.zeros((TOK, 256), F32)
    for e in range(BLK):
        hit = (places[e:e + 1, :] == spots) & (comb[e:e + 1, :] > 0)
        total += (
            lax.dot_general(jnp.where(hit, 1.0, 0.0).astype(BF), ret[e], TN, preferred_element_type=F32)
            * comb_t[:, e:e + 1]
        )
    mixed[...] = total.astype(BF)
    links.arrived(sc_id, sc_far)
    links.arrived(so_id, so_far)
    for d in (1, 2, 3, 0):
        rows = quarter(lax.rem(y - d + 4, 4))
        links.arrived(gd_ids["far", d], far_gd.at[rows])
        if d:
            links.arrived(gd_ids["own", d], own_gd.at[rows])
    links.finish()


def layer(*args):
    n = 160
    vm = pl.BlockSpec(memory_space=pltpu.VMEM)
    hbm = pl.BlockSpec(memory_space=pl.ANY)
    return pl.pallas_call(
        layer_kernel,
        out_shape=(
            jax.ShapeDtypeStruct((TOK, 256), BF),
            jax.ShapeDtypeStruct((256, D), BF),
            jax.ShapeDtypeStruct((2048, 256), BF),
            jax.ShapeDtypeStruct((2048, 256), BF),
            jax.ShapeDtypeStruct((8, 128), F32),
            jax.ShapeDtypeStruct((8, 128), F32),
            jax.ShapeDtypeStruct((8, 256), F32),
            jax.ShapeDtypeStruct((8, 256), F32),
        ),
        in_specs=[vm, vm, vm, hbm, hbm, hbm, vm, vm, vm, vm, vm],
        out_specs=[vm] * 8,
        scratch_shapes=[
            pltpu.VMEM((BLK, TOK, D), BF),
            pltpu.VMEM((D, 256), BF),
            pltpu.VMEM((BLK, TOK, 256), BF),
            pltpu.VMEM((BLK, BLK, TOK), F32),
            pltpu.VMEM((BLK, TOK), F32),
            pltpu.VMEM((BLK, TOK), F32),
            pltpu.VMEM((BLK, TOK), F32),
            pltpu.VMEM((ROWS, 256), BF),
            pltpu.VMEM((4, ROWS, 256), BF),
            pltpu.VMEM((4, 512, 256), BF),
            pltpu.VMEM((4, ROWS, 128), BF),
            pltpu.VMEM((3, ROWS, 128), BF),
            pltpu.VMEM((ROWS, 256), F32),
            pltpu.VMEM((ROWS, 128), BF),
            pltpu.VMEM((ROWS, 512), BF),
            pltpu.VMEM((512, ROWS), BF),
            pltpu.VMEM((4, ROWS, 256), BF),
            pltpu.VMEM((3, ROWS, 256), BF),
            pltpu.VMEM((ROWS, 256), BF),
            pltpu.VMEM((BLK, CAP, 256), BF),
            pltpu.VMEM((4, 512, 256), BF),
            pltpu.VMEM((ROWS, 256), BF),
            pltpu.VMEM((ROWS, 256), BF),
            pltpu.VMEM((256, BLK * TOK), BF),
            pltpu.SemaphoreType.DMA((n,)),
            pltpu.SemaphoreType.DMA((n,)),
            pltpu.SemaphoreType.DMA((3,)),
        ],
        name="layer",
        compiler_params=pltpu.CompilerParams(collective_id=0, has_side_effects=True, vmem_limit_bytes=VMEM_LIMIT),
    )(*args)


def per_device(
    tokens, cotangent, routes, router_weight, w_gate, w_up, w_down,
    scale_gate, scale_up, scale_down, swapped,
):
    me = lax.axis_index("expert")
    ids = jnp.arange(BLK, dtype=jnp.int32)
    flag = jnp.sum(jnp.where(ids == me, swapped, 0)) == 1
    comb_t = jnp.sum(jnp.where(routes[:, :, None] == ids, router_weight[:, :, None], 0.0), axis=1)
    mixed, grad_t, gd_own, gd_far, sc, sc_far, so_own, so_far = layer(
        comb_t.T, comb_t, cotangent, tokens, w_gate[0], w_up[0], w_down[0],
        scale_gate, scale_up, scale_down, jnp.where(flag, jnp.ones((1, 256), F32), 0.0),
    )
    wgrad = grad_t.T
    grad_down = jnp.where(flag, gd_far, gd_own)
    scale_in = jnp.where(flag, sc_far, sc)[0:2].astype(BF)
    scale_out = jnp.where(flag, so_far, so_own)[0:1].astype(BF)
    return mixed, wgrad[None, :, :128], wgrad[None, :, 128:], grad_down[None], scale_in[None], scale_out


def solution(mesh):
    in_specs = (
        P("expert", None),
        P("expert", "dp"),
        P("expert", None),
        P("expert", None),
        P("expert", None, "dp"),
        P("expert", None, "dp"),
        P("expert", None, "dp"),
        P("expert", "dp"),
        P("expert", "dp"),
        P("expert", "dp"),
        P(),
    )
    out_specs = (
        P("expert", "dp"),
        P("expert", None, "dp"),
        P("expert", None, "dp"),
        P("expert", None, "dp"),
        P("expert", None, "dp"),
        P("expert", "dp"),
    )
    return jax.shard_map(
        per_device, mesh=mesh, in_specs=in_specs, out_specs=out_specs, check_vma=False
    )
```

```python
import jax
import jax.numpy as jnp
from jax import lax
from jax.experimental import pallas as pl
from jax.experimental.pallas import tpu as pltpu
from jax.sharding import PartitionSpec as P

MESH = pl.DeviceIdType.MESH
BF = jnp.bfloat16
F32 = jnp.float32
CAP = 80
BLK = 16
TOK = 128
D = 4096
ROWS = BLK * CAP
CROWS = ROWS // 4
ORDER = (0, 1, 3, 2)
VMEM_LIMIT = 60 * 2**20
NT = (((1,), (1,)), ((), ()))
TN = (((0,), (0,)), ((), ()))


def place():
    dp = lax.axis_index("dp")
    ex = lax.axis_index("expert")
    y, zh = lax.div(dp, 4), lax.rem(dp, 4)
    x, zl, c = lax.div(ex, 4), lax.rem(lax.div(ex, 2), 2), lax.rem(ex, 2)
    return x, y, zh * 2 + zl, c


def device(x, y, z, c):
    x, y, z, c = lax.rem(x + 4, 4), lax.rem(y + 4, 4), lax.rem(z + 8, 8), lax.rem(c + 2, 2)
    return (y * 4 + lax.div(z, 2), slot(x, z, c))


def slot(x, z, c):
    return lax.rem(x + 4, 4) * 4 + lax.rem(z + 8, 2) * 2 + c


class Links:
    def __init__(self, send_sems, recv_sems, other):
        self.ss, self.rs, self.other = send_sems, recv_sems, other
        self.copies = []

    def send(self, src, dst, to):
        i = len(self.copies)
        copy = pltpu.make_async_remote_copy(
            src_ref=src,
            dst_ref=dst,
            send_sem=self.ss.at[i],
            recv_sem=self.rs.at[i],
            device_id=to,
            device_id_type=MESH,
        )
        copy.start()
        self.copies.append(copy)
        return i

    def arrived(self, i, dst):
        pltpu.make_async_remote_copy(
            src_ref=dst,
            dst_ref=dst,
            send_sem=self.ss.at[i],
            recv_sem=self.rs.at[i],
            device_id=self.other,
            device_id_type=MESH,
        ).wait_recv()

    def finish(self):
        for copy in self.copies:
            copy.wait_send()


def greet(devices):
    barrier = pltpu.get_barrier_semaphore()
    for to in devices:
        pl.semaphore_signal(barrier, inc=1, device_id=to, device_id_type=MESH)
    pl.semaphore_wait(barrier, len(devices))


def layer_kernel(
    routes, weights, cot, tok, wg, wu, wd, sg, su, sd, swapped,
    mixed, grad_gate, grad_up, grad_down, grad_in, grad_out,
    comb, comb_t, own_gd, far_gd, sc, sc_far, so, so_far,
    toks, w_in, cots, combs, cw_own, cw_par, pos, rg, di4, wd4, part, rz,
    pre, hid, hz, hz_t, op, ro, eo, ret, gd, gi, gi_far, spread_t, ss, rs, local,
):
    x, y, z, c = place()
    zl = lax.rem(z, 2)
    zh = lax.div(z, 2)
    me = slot(x, z, c)
    inner = lax.rem(me, 4)
    dp = lax.axis_index("dp")
    sibling = device(x, y, z, 1 - c)
    far = device(x + 2, y, z, c)
    up, down = device(x, y, z + 1, c), device(x, y, z - 1, c)
    chip = x * 2 + zl
    links = Links(ss, rs, sibling)

    def chip_at(k):
        q = lax.rem(chip + k + 8, 8)
        return lax.div(q, 2), zh * 2 + lax.rem(q, 2)

    def columns(j):
        return pl.ds(pl.multiple_of(j * 128, 128), 128)

    def quarter(j):
        return pl.ds(pl.multiple_of(j * 512, 512), 512)

    def chunk(j):
        return pl.ds(pl.multiple_of(j * CROWS, CROWS), CROWS)

    def block(r):
        return pl.ds(pl.multiple_of(r * CAP, CAP), CAP)

    loads = [
        pltpu.make_async_copy(tok, toks.at[me], local.at[0]),
        pltpu.make_async_copy(wg, w_in.at[:, pl.ds(0, 128)], local.at[1]),
        pltpu.make_async_copy(wu, w_in.at[:, pl.ds(128, 128)], local.at[2]),
    ]
    for load in loads:
        load.start()

    names = lax.broadcasted_iota(jnp.int32, (TOK, TOK), 0)
    dense = jnp.zeros((TOK, TOK), F32)
    for k in range(routes.shape[0]):
        dense += jnp.where(routes[k:k + 1, :] == names, weights[k:k + 1, :], 0.0)
    comb[...] = dense[0:BLK]
    comb_t[...] = dense.T

    peers = [(dp, lax.rem(me + k, 16)) for k in range(1, 16)]
    peers.append(device(x, y, z - 1 + 2 * zl, c))
    for d in range(1, 4):
        peers.append(device(x, y + d, z, c))
        peers.append(device(x, y, z + 2 * d, c))
        peers.append(device(x + 2, y + d, z, c))
    greet(peers)

    first = []
    for k in range(1, 8):
        qx, qz = chip_at(k)
        to = device(qx, y, qz, c)
        first.append((k, links.send(comb, combs.at[me], to), links.send(cot, cots.at[me], to)))
    over = [(0, links.send(comb, combs.at[me], sibling), links.send(cot, cots.at[me], sibling))]
    wd_ids = []
    for d in (1, 3, 2):
        wd_ids.append((d, links.send(wd.at[quarter(lax.rem(y + d, 4))], wd4.at[y], device(x, y + d, z, c))))

    lower, upper = pl.ds(0, 64), pl.ds(64, 64)
    halves = {"l": lower, "u": upper}
    pair = {}

    def to_sibling(d, dz, rows):
        s = slot(x - d, z + dz, c)
        pair.setdefault((d, dz), []).append((links.send(toks.at[s, rows], toks.at[s, rows], sibling), rows))

    z_ids, x_ids, f_ids = {}, {}, {}
    z_ids["l"] = links.send(tok.at[lower], toks.at[me, lower], up)
    z_ids["u"] = links.send(tok.at[upper], toks.at[me, upper], down)
    for d, h in ((1, "l"), (3, "u"), (1, "u"), (3, "l")):
        x_ids[d, 0, h] = links.send(tok.at[halves[h]], toks.at[me, halves[h]], device(x + d, y, z, c))
    pair[0, 0] = [(links.send(tok, toks.at[me], sibling), pl.ds(0, TOK))]

    combs[me] = comb[...]
    cots[me] = cot[...]
    wd4[y] = wd[quarter(y), :]
    for k, ia, ib in first:
        qx, qz = chip_at(-k)
        s = slot(qx, qz, c)
        links.arrived(ia, combs.at[s])
        links.arrived(ib, cots.at[s])
        over.append((k, links.send(combs.at[s], combs.at[s], sibling), links.send(cots.at[s], cots.at[s], sibling)))
    for k, ia, ib in over:
        qx, qz = chip_at(-k)
        s = slot(qx, qz, 1 - c)
        links.arrived(ia, combs.at[s])
        links.arrived(ib, cots.at[s])

    experts = lax.broadcasted_iota(jnp.int32, (BLK, BLK, TOK), 1)
    table = combs[...]
    cw = jnp.sum(jnp.where(experts == me, table, 0.0), axis=1)
    cw_own[...] = cw
    cw_par[...] = jnp.sum(jnp.where(experts == lax.rem(me + 8, 16), table, 0.0), axis=1)
    before = (
        lax.broadcasted_iota(jnp.int32, (TOK, TOK), 0) < lax.broadcasted_iota(jnp.int32, (TOK, TOK), 1)
    ).astype(F32).astype(BF)
    pos[...] = jnp.dot((cw > 0).astype(BF), before, preferred_element_type=F32)
    spots = lax.broadcasted_iota(jnp.int32, (CAP, TOK), 0).astype(F32)
    down_scale = sd[...].astype(F32)

    def compact(r, _):
        weight = cw_own[pl.ds(r, 1), :]
        hit = (pos[pl.ds(r, 1), :] == spots) & (weight > 0)
        picked = jnp.dot(jnp.where(hit, 1.0, 0.0).astype(BF), cots[r], preferred_element_type=F32)
        w = jnp.sum(jnp.where(hit, weight, 0.0), axis=1, keepdims=True)
        routed = (picked * w).astype(BF)
        rg[block(r), :] = routed
        di4[y, block(r), :] = (routed.astype(F32) * down_scale).astype(BF)
        return 0

    def rows_of(d, part=None):
        start = lax.rem(x - d + 4, 4) * CROWS
        if part is None:
            return pl.ds(pl.multiple_of(start, CROWS), CROWS)
        return pl.ds(pl.multiple_of(start + part * (CROWS // 2), CROWS // 2), CROWS // 2)

    y_ids = {}
    for g in ORDER:
        at = lax.rem(x - g + 4, 4) * 4
        lax.fori_loop(at, at + 4, compact, 0)
        rows = rows_of(g)
        for d in (1, 3):
            y_ids[g, d] = links.send(di4.at[y, rows], di4.at[y, rows], device(x, y + d, z, c))
    for d, i in wd_ids:
        links.arrived(i, wd4.at[lax.rem(y - d + 4, 4)])

    def y_fwd(g):
        for d, h in ((1, 0), (3, 1)):
            j = lax.rem(y - d + 4, 4)
            links.arrived(y_ids[g, d], di4.at[j, rows_of(g)])
            rows = rows_of(g, h)
            y_ids[g, d, "f"] = links.send(di4.at[j, rows], di4.at[j, rows], device(x, y + d, z, c))

    zr = {}

    def terms(g):
        rows = rows_of(g)
        for d, h in ((1, 0), (3, 1)):
            links.arrived(y_ids[g, d, "f"], di4.at[lax.rem(y + 2, 4), rows_of(g, h)])
        acc = lax.dot_general(di4[0, rows, :], wd4[0], NT, preferred_element_type=F32)
        for j in range(1, 4):
            acc += lax.dot_general(di4[j, rows, :], wd4[j], NT, preferred_element_type=F32)
        acc = acc.astype(BF)
        for j in range(4):
            part[j, rows, :] = acc[:, j * 128:(j + 1) * 128]
        for d in (2, 1, 3):
            zr[g, d] = links.send(part.at[lax.rem(zh + d, 4), rows], rz.at[d - 1, rows], device(x, y, z + 2 * d, c))

    def z_own():
        s = slot(x, z + 1, c)
        for h, order in (("l", (1, 3)), ("u", (3, 1))):
            rows = halves[h]
            links.arrived(z_ids[h], toks.at[s, rows])
            for d in order:
                x_ids[d, 1, h] = links.send(toks.at[s, rows], toks.at[s, rows], device(x + d, y, z, c))
            to_sibling(0, 1, rows)

    def x_first(dz):
        for d, h in ((1, "l"), (3, "u")):
            s = slot(x - d, z + dz, c)
            rows = halves[h]
            links.arrived(x_ids[d, dz, h], toks.at[s, rows])
            f_ids[d, dz] = links.send(toks.at[s, rows], toks.at[s, rows], device(x + d, y, z, c))
            to_sibling(d, dz, rows)

    def x_second(dz):
        for d, h in ((1, "u"), (3, "l")):
            s = slot(x - d, z + dz, c)
            links.arrived(x_ids[d, dz, h], toks.at[s, halves[h]])
            to_sibling(d, dz, halves[h])

    def x_far(dz):
        for d, h in ((1, "l"), (3, "u")):
            s = slot(x + 2, z + dz, c)
            links.arrived(f_ids[d, dz], toks.at[s, halves[h]])
            to_sibling(2, dz, halves[h])

    gate_scale = sg[...].astype(F32)
    up_scale = su[...].astype(F32)
    hid_ids = {}

    def group(d):
        gx = lax.rem(x - d + 4, 4)
        for dz in (0, 1):
            s = slot(x - d, z + dz, 1 - c)
            for i, rows in pair[d, dz]:
                links.arrived(i, toks.at[s, rows])

        def deepen(k, acc):
            at = pl.ds(pl.multiple_of(k * 1024, 1024), 1024)
            left = toks[pl.ds(gx * 4, 4), :, at].reshape(4 * TOK, 1024)
            return acc + jnp.dot(left, w_in[at, :], preferred_element_type=F32)

        acc = lax.fori_loop(0, 4, deepen, jnp.zeros((4 * TOK, 256), F32))
        for j in range(4):
            r = gx * 4 + j
            hit = (pos[pl.ds(r, 1), :] == spots) & (cw_own[pl.ds(r, 1), :] > 0)
            pre[block(r), :] = jnp.dot(
                jnp.where(hit, 1.0, 0.0), acc[j * TOK:(j + 1) * TOK], precision=lax.Precision.HIGHEST,
                preferred_element_type=F32,
            )
        rows = chunk(gx)
        gate_act = pre[rows, 0:128] * gate_scale
        up_act = pre[rows, 128:256] * up_scale
        hid[rows, :] = (gate_act * jax.nn.sigmoid(gate_act) * up_act).astype(BF)
        hz[rows, columns(zh)] = hid[rows, :]
        for dz in (1, 3):
            hid_ids[d, dz] = links.send(hid.at[rows], hz.at[rows, columns(zh)], device(x, y, z + 2 * dz, c))

    def hid_fwd(d):
        for dz, h in ((1, 0), (3, 1)):
            at = columns(lax.rem(zh - dz + 4, 4))
            links.arrived(hid_ids[d, dz], hz.at[rows_of(d), at])
            rows = rows_of(d, h)
            hid_ids[d, dz, "f"] = links.send(hz.at[rows, at], hz.at[rows, at], device(x, y, z + 2 * dz, c))

    out_ids = {}

    def project(d):
        rows = chunk(lax.rem(x - d + 4, 4))
        for dz, h in ((1, 0), (3, 1)):
            links.arrived(hid_ids[d, dz, "f"], hz.at[rows_of(d, h), columns(lax.rem(zh + 2, 4))])
        left = hz[rows, :]
        hz_t[lax.rem(x - d + 4, 4)] = left.T
        for dy in (2, 1, 3, 0):
            j = lax.rem(y + dy, 4)
            op[j, rows, :] = jnp.dot(left, wd4[j], preferred_element_type=F32).astype(BF)
            if dy:
                out_ids[d, dy] = links.send(op.at[j, rows], ro.at[dy - 1, rows], device(x, y + dy, z, c))

    so[...] = jnp.zeros_like(so)
    back = {}

    def give(d):
        gx = lax.rem(x - d + 4, 4)
        rows = chunk(gx)
        for dy in (1, 3, 2):
            links.arrived(out_ids[d, dy], ro.at[dy - 1, rows])
        total = op[y, rows, :].astype(F32)
        for dy in (1, 2, 3):
            total += ro[dy - 1, rows, :].astype(F32)
        so[0:1, :] += jnp.sum(total * rg[rows, :].astype(F32), axis=0, keepdims=True)
        eo[rows, :] = (total * down_scale).astype(BF)
        for j in range(4):
            r = gx * 4 + lax.rem(inner + j, 4)
            if d == 0 and j == 0:
                ret[me] = eo[block(r), :]
            else:
                back[d, j] = links.send(eo.at[block(r)], ret.at[me], (dp, r))

    sc[...] = jnp.zeros_like(sc)
    gi_ids = {}

    def gradient(g):
        rows = rows_of(g)
        for d in (1, 2, 3):
            links.arrived(zr[g, d], rz.at[d - 1, rows])
        total = part[zh, rows, :].astype(F32)
        for d in (1, 2, 3):
            total += rz[d - 1, rows, :].astype(F32)
        gate_pre, up_pre = pre[rows, 0:128], pre[rows, 128:256]
        gate_act, up_act = gate_pre * gate_scale, up_pre * up_scale
        sig = jax.nn.sigmoid(gate_act)
        gate_grad = total * up_act * sig * (1.0 + gate_act * (1.0 - sig))
        up_grad = total * (gate_act * sig)
        sc[0:1, :] += jnp.sum(gate_grad * gate_pre, axis=0, keepdims=True)
        sc[1:2, :] += jnp.sum(up_grad * up_pre, axis=0, keepdims=True)
        gi[rows, 0:128] = (gate_grad * gate_scale).astype(BF)
        gi[rows, 128:256] = (up_grad * up_scale).astype(BF)

    def trade_gi(g):
        gi_ids[g] = links.send(gi.at[rows_of(g)], gi_far.at[rows_of(g)], far)

    for load in loads:
        load.wait()
    z_own()
    y_fwd(0)
    group(0)
    x_first(0)
    y_fwd(1)
    terms(0)
    y_fwd(3)
    x_second(0)
    terms(1)
    hid_fwd(0)
    y_fwd(2)
    x_first(1)
    terms(3)
    terms(2)
    project(0)
    x_second(1)
    x_far(0)
    group(1)
    group(3)
    hid_fwd(1)
    hid_fwd(3)
    gradient(0)
    give(0)
    gradient(1)
    project(1)
    gradient(3)
    project(3)
    x_far(1)
    for g in (0, 1, 3):
        trade_gi(g)
    group(2)
    give(1)
    hid_fwd(2)
    gradient(2)
    project(2)

    gd_ids = {}
    for d in (2, 1, 3, 0):
        j = lax.rem(y + d, 4)
        acc = jnp.dot(hz_t[0], di4[j, 0:CROWS, :], preferred_element_type=F32)
        for i in range(1, 4):
            acc += jnp.dot(hz_t[i], di4[j, i * CROWS:(i + 1) * CROWS, :], preferred_element_type=F32)
        gd[j] = acc.astype(BF)
        gd_ids["far", d] = links.send(gd.at[j], far_gd.at[quarter(y)], device(x + 2, y + d, z, c))
        if d:
            gd_ids["own", d] = links.send(gd.at[j], own_gd.at[quarter(y)], device(x, y + d, z, c))
        else:
            own_gd[quarter(y), :] = gd[j]
    trade_gi(2)
    sc_id = links.send(sc, sc_far, far)
    give(3)
    give(2)
    so_id = links.send(so, so_far, far)

    for g in ORDER:
        links.arrived(gi_ids[g], gi_far.at[rows_of((g + 2) % 4)])
    trade = jnp.sum(jnp.where(lax.broadcasted_iota(jnp.int32, (1, BLK), 1) == me, swapped[...], 0), axis=1, keepdims=True) > 0
    cw_sel = jnp.where(trade, cw_par[...], cw_own[...])
    cw_par[...] = cw_sel
    pos[...] = jnp.dot((cw_sel > 0).astype(BF), before, preferred_element_type=F32)

    def expand(r, _):
        hit = (pos[pl.ds(r, 1), :] == spots) & (cw_par[pl.ds(r, 1), :] > 0)
        chosen = jnp.where(trade, gi_far[block(r), :].astype(F32), gi[block(r), :].astype(F32)).astype(BF)
        spread_t[:, columns(r)] = lax.dot_general(
            chosen, jnp.where(hit, 1.0, 0.0).astype(BF), TN, preferred_element_type=F32
        ).astype(BF)
        return 0

    lax.fori_loop(0, BLK, expand, 0)

    def weight_grad(k, _):
        at = pl.ds(pl.multiple_of(k * 512, 512), 512)
        right = toks[:, :, at].reshape(BLK * TOK, 512)
        grad = jnp.dot(spread_t[...], right, preferred_element_type=F32).astype(BF).T
        grad_gate[at, :] = grad[:, 0:128]
        grad_up[at, :] = grad[:, 128:256]
        return 0

    lax.fori_loop(0, D // 512, weight_grad, 0)

    for (d, j), k in back.items():
        links.arrived(k, ret.at[lax.rem(x + d, 4) * 4 + lax.rem(inner + 4 - j, 4)])
    places = jnp.dot((comb[...] > 0).astype(BF), before, preferred_element_type=F32)
    total = jnp.zeros((TOK, 256), F32)
    for e in range(BLK):
        hit = (places[e:e + 1, :] == spots) & (comb[e:e + 1, :] > 0)
        total += (
            lax.dot_general(jnp.where(hit, 1.0, 0.0).astype(BF), ret[e], TN, preferred_element_type=F32)
            * comb_t[:, e:e + 1]
        )
    mixed[...] = total.astype(BF)
    links.arrived(sc_id, sc_far)
    links.arrived(so_id, so_far)
    for d in (1, 2, 3, 0):
        rows = quarter(lax.rem(y - d + 4, 4))
        links.arrived(gd_ids["far", d], far_gd.at[rows])
        if d:
            links.arrived(gd_ids["own", d], own_gd.at[rows])
    grad_down[...] = jnp.where(trade, far_gd[...], own_gd[...])
    grad_in[...] = jnp.where(trade, sc_far[0:2], sc[0:2]).astype(BF)
    grad_out[...] = jnp.where(trade, so_far[0:1], so[0:1]).astype(BF)
    links.finish()


def layer(*args):
    n = 160
    vm = pl.BlockSpec(memory_space=pltpu.VMEM)
    hbm = pl.BlockSpec(memory_space=pl.ANY)
    return pl.pallas_call(
        layer_kernel,
        out_shape=(
            jax.ShapeDtypeStruct((TOK, 256), BF),
            jax.ShapeDtypeStruct((D, 128), BF),
            jax.ShapeDtypeStruct((D, 128), BF),
            jax.ShapeDtypeStruct((2048, 256), BF),
            jax.ShapeDtypeStruct((2, 128), BF),
            jax.ShapeDtypeStruct((1, 256), BF),
        ),
        in_specs=[vm, vm, vm, hbm, hbm, hbm, vm, vm, vm, vm, vm],
        out_specs=[vm] * 6,
        scratch_shapes=[
            pltpu.VMEM((BLK, TOK), F32),
            pltpu.VMEM((TOK, TOK), F32),
            pltpu.VMEM((2048, 256), BF),
            pltpu.VMEM((2048, 256), BF),
            pltpu.VMEM((8, 128), F32),
            pltpu.VMEM((8, 128), F32),
            pltpu.VMEM((8, 256), F32),
            pltpu.VMEM((8, 256), F32),
            pltpu.VMEM((BLK, TOK, D), BF),
            pltpu.VMEM((D, 256), BF),
            pltpu.VMEM((BLK, TOK, 256), BF),
            pltpu.VMEM((BLK, BLK, TOK), F32),
            pltpu.VMEM((BLK, TOK), F32),
            pltpu.VMEM((BLK, TOK), F32),
            pltpu.VMEM((BLK, TOK), F32),
            pltpu.VMEM((ROWS, 256), BF),
            pltpu.VMEM((4, ROWS, 256), BF),
            pltpu.VMEM((4, 512, 256), BF),
            pltpu.VMEM((4, ROWS, 128), BF),
            pltpu.VMEM((3, ROWS, 128), BF),
            pltpu.VMEM((ROWS, 256), F32),
            pltpu.VMEM((ROWS, 128), BF),
            pltpu.VMEM((ROWS, 512), BF),
            pltpu.VMEM((4, 512, CROWS), BF),
            pltpu.VMEM((4, ROWS, 256), BF),
            pltpu.VMEM((3, ROWS, 256), BF),
            pltpu.VMEM((ROWS, 256), BF),
            pltpu.VMEM((BLK, CAP, 256), BF),
            pltpu.VMEM((4, 512, 256), BF),
            pltpu.VMEM((ROWS, 256), BF),
            pltpu.VMEM((ROWS, 256), BF),
            pltpu.VMEM((256, BLK * TOK), BF),
            pltpu.SemaphoreType.DMA((n,)),
            pltpu.SemaphoreType.DMA((n,)),
            pltpu.SemaphoreType.DMA((3,)),
        ],
        name="layer",
        compiler_params=pltpu.CompilerParams(collective_id=0, has_side_effects=True, vmem_limit_bytes=VMEM_LIMIT),
    )(*args)


def per_device(
    tokens, cotangent, routes, router_weight, w_gate, w_up, w_down,
    scale_gate, scale_up, scale_down, swapped,
):
    mixed, grad_gate, grad_up, grad_down, grad_in, grad_out = layer(
        routes.T, router_weight.T, cotangent, tokens, w_gate[0], w_up[0], w_down[0],
        scale_gate, scale_up, scale_down, swapped[None],
    )
    return mixed, grad_gate[None], grad_up[None], grad_down[None], grad_in[None], grad_out


def solution(mesh):
    in_specs = (
        P("expert", None),
        P("expert", "dp"),
        P("expert", None),
        P("expert", None),
        P("expert", None, "dp"),
        P("expert", None, "dp"),
        P("expert", None, "dp"),
        P("expert", "dp"),
        P("expert", "dp"),
        P("expert", "dp"),
        P(),
    )
    out_specs = (
        P("expert", "dp"),
        P("expert", None, "dp"),
        P("expert", None, "dp"),
        P("expert", None, "dp"),
        P("expert", None, "dp"),
        P("expert", "dp"),
    )
    return jax.shard_map(
        per_device, mesh=mesh, in_specs=in_specs, out_specs=out_specs, check_vma=False
    )
```

```python
import jax
import jax.numpy as jnp
from jax import lax
from jax.experimental import pallas as pl
from jax.experimental.pallas import tpu as pltpu
from jax.sharding import PartitionSpec as P

MESH = pl.DeviceIdType.MESH
BF = jnp.bfloat16
F32 = jnp.float32
CAP = 80
BLK = 16
TOK = 128
D = 4096
ROWS = BLK * CAP
CROWS = ROWS // 4
ORDER = (0, 1, 3, 2)
XCOLS = 1280
YCOLS = 384
VMEM_LIMIT = 60 * 2**20
NT = (((1,), (1,)), ((), ()))
TN = (((0,), (0,)), ((), ()))


def place():
    dp = lax.axis_index("dp")
    ex = lax.axis_index("expert")
    y, zh = lax.div(dp, 4), lax.rem(dp, 4)
    x, zl, c = lax.div(ex, 4), lax.rem(lax.div(ex, 2), 2), lax.rem(ex, 2)
    return x, y, zh * 2 + zl, c


def device(x, y, z, c):
    x, y, z, c = lax.rem(x + 4, 4), lax.rem(y + 4, 4), lax.rem(z + 8, 8), lax.rem(c + 2, 2)
    return (y * 4 + lax.div(z, 2), slot(x, z, c))


def slot(x, z, c):
    return lax.rem(x + 4, 4) * 4 + lax.rem(z + 8, 2) * 2 + c


class Links:
    def __init__(self, send_sems, recv_sems, other):
        self.ss, self.rs, self.other = send_sems, recv_sems, other
        self.copies = []

    def send(self, src, dst, to):
        i = len(self.copies)
        copy = pltpu.make_async_remote_copy(
            src_ref=src,
            dst_ref=dst,
            send_sem=self.ss.at[i],
            recv_sem=self.rs.at[i],
            device_id=to,
            device_id_type=MESH,
        )
        copy.start()
        self.copies.append(copy)
        return i

    def arrived(self, i, dst):
        pltpu.make_async_remote_copy(
            src_ref=dst,
            dst_ref=dst,
            send_sem=self.ss.at[i],
            recv_sem=self.rs.at[i],
            device_id=self.other,
            device_id_type=MESH,
        ).wait_recv()

    def finish(self):
        for copy in self.copies:
            copy.wait_send()


def greet(devices):
    barrier = pltpu.get_barrier_semaphore()
    for to in devices:
        pl.semaphore_signal(barrier, inc=1, device_id=to, device_id_type=MESH)
    pl.semaphore_wait(barrier, len(devices))


def layer_kernel(
    routes, weights, cot, tok, wg, wu, wd, sg, su, sd, swapped,
    mixed, grad_gate, grad_up, grad_down, grad_in, grad_out,
    comb, comb_t, own_gd, far_gd, sc, sc_far, so, so_far,
    toks, w_in, cots, combs, cw_own, cw_par, pos, rg, di4, wd4, part, rz,
    pre, hid, hz, hz_t, op, ro, eo, ret, gd, gi, gi_far, spread_t, ss, rs, local,
):
    x, y, z, c = place()
    zl = lax.rem(z, 2)
    zh = lax.div(z, 2)
    me = slot(x, z, c)
    inner = lax.rem(me, 4)
    dp = lax.axis_index("dp")
    sibling = device(x, y, z, 1 - c)
    far = device(x + 2, y, z, c)
    up, down = device(x, y, z + 1, c), device(x, y, z - 1, c)
    chip = x * 2 + zl
    links = Links(ss, rs, sibling)

    def chip_at(k):
        q = lax.rem(chip + k + 8, 8)
        return lax.div(q, 2), zh * 2 + lax.rem(q, 2)

    def columns(j):
        return pl.ds(pl.multiple_of(j * 128, 128), 128)

    def quarter(j):
        return pl.ds(pl.multiple_of(j * 512, 512), 512)

    def chunk(j):
        return pl.ds(pl.multiple_of(j * CROWS, CROWS), CROWS)

    def block(r):
        return pl.ds(pl.multiple_of(r * CAP, CAP), CAP)

    loads = [
        pltpu.make_async_copy(tok, toks.at[me], local.at[0]),
        pltpu.make_async_copy(wg, w_in.at[:, pl.ds(0, 128)], local.at[1]),
        pltpu.make_async_copy(wu, w_in.at[:, pl.ds(128, 128)], local.at[2]),
    ]
    for load in loads:
        load.start()

    names = lax.broadcasted_iota(jnp.int32, (TOK, TOK), 0)
    dense = jnp.zeros((TOK, TOK), F32)
    for k in range(routes.shape[0]):
        dense += jnp.where(routes[k:k + 1, :] == names, weights[k:k + 1, :], 0.0)
    comb[...] = dense[0:BLK]
    comb_t[...] = dense.T

    peers = [(dp, lax.rem(me + k, 16)) for k in range(1, 16)]
    peers.append(device(x, y, z - 1 + 2 * zl, c))
    for d in range(1, 4):
        peers.append(device(x, y + d, z, c))
        peers.append(device(x, y, z + 2 * d, c))
        peers.append(device(x + 2, y + d, z, c))
    greet(peers)

    first = []
    for k in range(1, 8):
        qx, qz = chip_at(k)
        to = device(qx, y, qz, c)
        first.append((k, links.send(comb, combs.at[me], to), links.send(cot, cots.at[me], to)))
    over = [(0, links.send(comb, combs.at[me], sibling), links.send(cot, cots.at[me], sibling))]
    wd_ids = []
    for d in (1, 3, 2):
        wd_ids.append((d, links.send(wd.at[quarter(lax.rem(y + d, 4))], wd4.at[y], device(x, y + d, z, c))))

    cols = {"l": pl.ds(0, XCOLS), "u": pl.ds(XCOLS, XCOLS)}
    ylow, yhigh = pl.ds(2 * XCOLS, 2 * YCOLS), pl.ds(2 * XCOLS + 2 * YCOLS, 2 * YCOLS)
    shared = pl.ds(2 * XCOLS, 4 * YCOLS)

    def mine(d):
        return pl.ds(pl.multiple_of(2 * XCOLS + lax.rem(y + d + 4, 4) * YCOLS, 128), YCOLS)

    pair = {}

    def to_sibling(d, dz, at):
        s = slot(x - d, z + dz, c)
        pair.setdefault((d, dz), []).append((links.send(toks.at[s, :, at], toks.at[s, :, at], sibling), at))

    z_ids, x_ids, f_ids, v_ids = {}, {}, {}, {}
    for name, at, to in (("l", cols["l"], up), ("u", cols["u"], down), ("ylow", ylow, up), ("yhigh", yhigh, down)):
        z_ids[name] = links.send(tok.at[:, at], toks.at[me, :, at], to)
    for d, h in ((1, "l"), (3, "u"), (1, "q"), (3, "q"), (1, "u"), (3, "l")):
        at = mine(0) if h == "q" else cols[h]
        x_ids[d, 0, h] = links.send(tok.at[:, at], toks.at[me, :, at], device(x + d, y, z, c))
    pair[0, 0] = [(links.send(tok, toks.at[me], sibling), pl.ds(0, D))]

    combs[me] = comb[...]
    cots[me] = cot[...]
    wd4[y] = wd[quarter(y), :]
    for k, ia, ib in first:
        qx, qz = chip_at(-k)
        s = slot(qx, qz, c)
        links.arrived(ia, combs.at[s])
        links.arrived(ib, cots.at[s])
        over.append((k, links.send(combs.at[s], combs.at[s], sibling), links.send(cots.at[s], cots.at[s], sibling)))
    for k, ia, ib in over:
        qx, qz = chip_at(-k)
        s = slot(qx, qz, 1 - c)
        links.arrived(ia, combs.at[s])
        links.arrived(ib, cots.at[s])

    experts = lax.broadcasted_iota(jnp.int32, (BLK, BLK, TOK), 1)
    table = combs[...]
    cw = jnp.sum(jnp.where(experts == me, table, 0.0), axis=1)
    cw_own[...] = cw
    cw_par[...] = jnp.sum(jnp.where(experts == lax.rem(me + 8, 16), table, 0.0), axis=1)
    before = (
        lax.broadcasted_iota(jnp.int32, (TOK, TOK), 0) < lax.broadcasted_iota(jnp.int32, (TOK, TOK), 1)
    ).astype(F32).astype(BF)
    pos[...] = jnp.dot((cw > 0).astype(BF), before, preferred_element_type=F32)
    spots = lax.broadcasted_iota(jnp.int32, (CAP, TOK), 0).astype(F32)
    down_scale = sd[...].astype(F32)

    def compact(r, _):
        weight = cw_own[pl.ds(r, 1), :]
        hit = (pos[pl.ds(r, 1), :] == spots) & (weight > 0)
        picked = jnp.dot(jnp.where(hit, 1.0, 0.0).astype(BF), cots[r], preferred_element_type=F32)
        w = jnp.sum(jnp.where(hit, weight, 0.0), axis=1, keepdims=True)
        routed = (picked * w).astype(BF)
        rg[block(r), :] = routed
        di4[y, block(r), :] = (routed.astype(F32) * down_scale).astype(BF)
        return 0

    def rows_of(d, part=None):
        start = lax.rem(x - d + 4, 4) * CROWS
        if part is None:
            return pl.ds(pl.multiple_of(start, CROWS), CROWS)
        return pl.ds(pl.multiple_of(start + part * (CROWS // 2), CROWS // 2), CROWS // 2)

    y_ids = {}
    for g in ORDER:
        at = lax.rem(x - g + 4, 4) * 4
        lax.fori_loop(at, at + 4, compact, 0)
        rows = rows_of(g)
        for d in (1, 3):
            y_ids[g, d] = links.send(di4.at[y, rows], di4.at[y, rows], device(x, y + d, z, c))
    for d, i in wd_ids:
        links.arrived(i, wd4.at[lax.rem(y - d + 4, 4)])

    def y_fwd(g):
        for d, h in ((1, 0), (3, 1)):
            j = lax.rem(y - d + 4, 4)
            links.arrived(y_ids[g, d], di4.at[j, rows_of(g)])
            rows = rows_of(g, h)
            y_ids[g, d, "f"] = links.send(di4.at[j, rows], di4.at[j, rows], device(x, y + d, z, c))

    zr = {}

    def terms(g):
        rows = rows_of(g)
        for d, h in ((1, 0), (3, 1)):
            links.arrived(y_ids[g, d, "f"], di4.at[lax.rem(y + 2, 4), rows_of(g, h)])
        acc = lax.dot_general(di4[0, rows, :], wd4[0], NT, preferred_element_type=F32)
        for j in range(1, 4):
            acc += lax.dot_general(di4[j, rows, :], wd4[j], NT, preferred_element_type=F32)
        acc = acc.astype(BF)
        for j in range(4):
            part[j, rows, :] = acc[:, j * 128:(j + 1) * 128]
        for d in (2, 1, 3):
            zr[g, d] = links.send(part.at[lax.rem(zh + d, 4), rows], rz.at[d - 1, rows], device(x, y, z + 2 * d, c))

    def z_own():
        s = slot(x, z + 1, c)
        for name, at in (("l", cols["l"]), ("u", cols["u"]), ("ylow", ylow), ("yhigh", yhigh)):
            links.arrived(z_ids[name], toks.at[s, :, at])
        for d, h in ((1, "l"), (3, "u"), (1, "q"), (3, "q"), (1, "u"), (3, "l")):
            at = mine(0) if h == "q" else cols[h]
            x_ids[d, 1, h] = links.send(toks.at[s, :, at], toks.at[s, :, at], device(x + d, y, z, c))
        to_sibling(0, 1, pl.ds(0, D))

    def x_first(dz):
        for d, h in ((1, "l"), (3, "u")):
            s = slot(x - d, z + dz, c)
            at = cols[h]
            links.arrived(x_ids[d, dz, h], toks.at[s, :, at])
            f_ids[d, dz] = links.send(toks.at[s, :, at], toks.at[s, :, at], device(x + d, y, z, c))
            to_sibling(d, dz, at)

    def x_second(dz):
        for d, h in ((1, "u"), (3, "l")):
            s = slot(x - d, z + dz, c)
            links.arrived(x_ids[d, dz, h], toks.at[s, :, cols[h]])
            to_sibling(d, dz, cols[h])

    def x_far(dz):
        for d, h in ((1, "l"), (3, "u")):
            s = slot(x + 2, z + dz, c)
            links.arrived(f_ids[d, dz], toks.at[s, :, cols[h]])
            to_sibling(2, dz, cols[h])

    def share(d, dz):
        view = toks.at[slot(x - d, z + dz, c), :, mine(0)]
        for dy in (1, 3):
            v_ids[d, dz, dy] = links.send(view, view, device(x, y + dy, z, c))

    def q_near(dz):
        for d in (1, 3):
            view = toks.at[slot(x - d, z + dz, c), :, mine(0)]
            links.arrived(x_ids[d, dz, "q"], view)
            if d == 1 + 2 * dz:
                f_ids["q", dz] = links.send(view, view, device(x + d, y, z, c))
            share(d, dz)

    def q_far(dz):
        links.arrived(f_ids["q", dz], toks.at[slot(x + 2, z + dz, c), :, mine(0)])
        share(2, dz)

    def v_pass(d, dz):
        s = slot(x - d, z + dz, c)
        for dy in (1, 3):
            view = toks.at[s, :, mine(-dy)]
            links.arrived(v_ids[d, dz, dy], view)
            if dy == 1 + 2 * dz:
                v_ids[d, dz, "f"] = links.send(view, view, device(x, y + dy, z, c))

    def v_last(d, dz):
        links.arrived(v_ids[d, dz, "f"], toks.at[slot(x - d, z + dz, c), :, mine(2)])
        to_sibling(d, dz, shared)

    gate_scale = sg[...].astype(F32)
    up_scale = su[...].astype(F32)
    hid_ids = {}

    def group(d):
        gx = lax.rem(x - d + 4, 4)
        for dz in (0, 1):
            s = slot(x - d, z + dz, 1 - c)
            for i, at in pair[d, dz]:
                links.arrived(i, toks.at[s, :, at])

        def deepen(k, acc):
            at = pl.ds(pl.multiple_of(k * 1024, 1024), 1024)
            left = toks[pl.ds(gx * 4, 4), :, at].reshape(4 * TOK, 1024)
            return acc + jnp.dot(left, w_in[at, :], preferred_element_type=F32)

        acc = lax.fori_loop(0, 4, deepen, jnp.zeros((4 * TOK, 256), F32))
        for j in range(4):
            r = gx * 4 + j
            hit = (pos[pl.ds(r, 1), :] == spots) & (cw_own[pl.ds(r, 1), :] > 0)
            pre[block(r), :] = jnp.dot(
                jnp.where(hit, 1.0, 0.0), acc[j * TOK:(j + 1) * TOK], precision=lax.Precision.HIGHEST,
                preferred_element_type=F32,
            )
        rows = chunk(gx)
        gate_act = pre[rows, 0:128] * gate_scale
        up_act = pre[rows, 128:256] * up_scale
        hid[rows, :] = (gate_act * jax.nn.sigmoid(gate_act) * up_act).astype(BF)
        hz[rows, columns(zh)] = hid[rows, :]
        for dz in (1, 3):
            hid_ids[d, dz] = links.send(hid.at[rows], hz.at[rows, columns(zh)], device(x, y, z + 2 * dz, c))

    def hid_fwd(d):
        for dz, h in ((1, 0), (3, 1)):
            at = columns(lax.rem(zh - dz + 4, 4))
            links.arrived(hid_ids[d, dz], hz.at[rows_of(d), at])
            rows = rows_of(d, h)
            hid_ids[d, dz, "f"] = links.send(hz.at[rows, at], hz.at[rows, at], device(x, y, z + 2 * dz, c))

    out_ids = {}

    def project(d):
        rows = chunk(lax.rem(x - d + 4, 4))
        for dz, h in ((1, 0), (3, 1)):
            links.arrived(hid_ids[d, dz, "f"], hz.at[rows_of(d, h), columns(lax.rem(zh + 2, 4))])
        left = hz[rows, :]
        hz_t[lax.rem(x - d + 4, 4)] = left.T
        for dy in (2, 1, 3, 0):
            j = lax.rem(y + dy, 4)
            op[j, rows, :] = jnp.dot(left, wd4[j], preferred_element_type=F32).astype(BF)
            if dy:
                out_ids[d, dy] = links.send(op.at[j, rows], ro.at[dy - 1, rows], device(x, y + dy, z, c))

    so[...] = jnp.zeros_like(so)
    back = {}

    def give(d):
        gx = lax.rem(x - d + 4, 4)
        rows = chunk(gx)
        for dy in (1, 3, 2):
            links.arrived(out_ids[d, dy], ro.at[dy - 1, rows])
        total = op[y, rows, :].astype(F32)
        for dy in (1, 2, 3):
            total += ro[dy - 1, rows, :].astype(F32)
        so[0:1, :] += jnp.sum(total * rg[rows, :].astype(F32), axis=0, keepdims=True)
        eo[rows, :] = (total * down_scale).astype(BF)
        for j in range(4):
            r = gx * 4 + lax.rem(inner + j, 4)
            if d == 0 and j == 0:
                ret[me] = eo[block(r), :]
            else:
                back[d, j] = links.send(eo.at[block(r)], ret.at[me], (dp, r))

    sc[...] = jnp.zeros_like(sc)
    gi_ids = {}

    def gradient(g):
        rows = rows_of(g)
        for d in (1, 2, 3):
            links.arrived(zr[g, d], rz.at[d - 1, rows])
        total = part[zh, rows, :].astype(F32)
        for d in (1, 2, 3):
            total += rz[d - 1, rows, :].astype(F32)
        gate_pre, up_pre = pre[rows, 0:128], pre[rows, 128:256]
        gate_act, up_act = gate_pre * gate_scale, up_pre * up_scale
        sig = jax.nn.sigmoid(gate_act)
        gate_grad = total * up_act * sig * (1.0 + gate_act * (1.0 - sig))
        up_grad = total * (gate_act * sig)
        sc[0:1, :] += jnp.sum(gate_grad * gate_pre, axis=0, keepdims=True)
        sc[1:2, :] += jnp.sum(up_grad * up_pre, axis=0, keepdims=True)
        gi[rows, 0:128] = (gate_grad * gate_scale).astype(BF)
        gi[rows, 128:256] = (up_grad * up_scale).astype(BF)

    def trade_gi(g):
        gi_ids[g] = links.send(gi.at[rows_of(g)], gi_far.at[rows_of(g)], far)

    for load in loads:
        load.wait()
    z_own()
    y_fwd(0)
    group(0)
    x_first(0)
    q_near(0)
    y_fwd(1)
    terms(0)
    q_far(0)
    v_pass(1, 0)
    v_pass(3, 0)
    y_fwd(3)
    x_second(0)
    terms(1)
    hid_fwd(0)
    y_fwd(2)
    x_first(1)
    q_near(1)
    v_pass(2, 0)
    terms(3)
    q_far(1)
    v_last(1, 0)
    v_last(3, 0)
    v_last(2, 0)
    v_pass(1, 1)
    v_pass(3, 1)
    terms(2)
    project(0)
    x_second(1)
    v_pass(2, 1)
    v_last(1, 1)
    v_last(3, 1)
    x_far(0)
    group(1)
    group(3)
    hid_fwd(1)
    hid_fwd(3)
    v_last(2, 1)
    gradient(0)
    give(0)
    gradient(1)
    project(1)
    gradient(3)
    project(3)
    x_far(1)
    for g in (0, 1, 3):
        trade_gi(g)
    group(2)
    give(1)
    hid_fwd(2)
    gradient(2)
    project(2)

    gd_ids = {}
    for d in (2, 1, 3, 0):
        j = lax.rem(y + d, 4)
        acc = jnp.dot(hz_t[0], di4[j, 0:CROWS, :], preferred_element_type=F32)
        for i in range(1, 4):
            acc += jnp.dot(hz_t[i], di4[j, i * CROWS:(i + 1) * CROWS, :], preferred_element_type=F32)
        gd[j] = acc.astype(BF)
        gd_ids["far", d] = links.send(gd.at[j], far_gd.at[quarter(y)], device(x + 2, y + d, z, c))
        if d:
            gd_ids["own", d] = links.send(gd.at[j], own_gd.at[quarter(y)], device(x, y + d, z, c))
        else:
            own_gd[quarter(y), :] = gd[j]
    trade_gi(2)
    sc_id = links.send(sc, sc_far, far)
    give(3)
    give(2)
    so_id = links.send(so, so_far, far)

    for g in ORDER:
        links.arrived(gi_ids[g], gi_far.at[rows_of((g + 2) % 4)])
    trade = jnp.sum(jnp.where(lax.broadcasted_iota(jnp.int32, (1, BLK), 1) == me, swapped[...], 0), axis=1, keepdims=True) > 0
    cw_sel = jnp.where(trade, cw_par[...], cw_own[...])
    cw_par[...] = cw_sel
    pos[...] = jnp.dot((cw_sel > 0).astype(BF), before, preferred_element_type=F32)

    def expand(r, _):
        hit = (pos[pl.ds(r, 1), :] == spots) & (cw_par[pl.ds(r, 1), :] > 0)
        chosen = jnp.where(trade, gi_far[block(r), :].astype(F32), gi[block(r), :].astype(F32)).astype(BF)
        spread_t[:, columns(r)] = lax.dot_general(
            chosen, jnp.where(hit, 1.0, 0.0).astype(BF), TN, preferred_element_type=F32
        ).astype(BF)
        return 0

    lax.fori_loop(0, BLK, expand, 0)

    def weight_grad(k, _):
        at = pl.ds(pl.multiple_of(k * 512, 512), 512)
        right = toks[:, :, at].reshape(BLK * TOK, 512)
        grad = jnp.dot(spread_t[...], right, preferred_element_type=F32).astype(BF).T
        grad_gate[at, :] = grad[:, 0:128]
        grad_up[at, :] = grad[:, 128:256]
        return 0

    lax.fori_loop(0, D // 512, weight_grad, 0)

    for (d, j), k in back.items():
        links.arrived(k, ret.at[lax.rem(x + d, 4) * 4 + lax.rem(inner + 4 - j, 4)])
    places = jnp.dot((comb[...] > 0).astype(BF), before, preferred_element_type=F32)
    total = jnp.zeros((TOK, 256), F32)
    for e in range(BLK):
        hit = (places[e:e + 1, :] == spots) & (comb[e:e + 1, :] > 0)
        total += (
            lax.dot_general(jnp.where(hit, 1.0, 0.0).astype(BF), ret[e], TN, preferred_element_type=F32)
            * comb_t[:, e:e + 1]
        )
    mixed[...] = total.astype(BF)
    links.arrived(sc_id, sc_far)
    links.arrived(so_id, so_far)
    for d in (1, 2, 3, 0):
        rows = quarter(lax.rem(y - d + 4, 4))
        links.arrived(gd_ids["far", d], far_gd.at[rows])
        if d:
            links.arrived(gd_ids["own", d], own_gd.at[rows])
    grad_down[...] = jnp.where(trade, far_gd[...], own_gd[...])
    grad_in[...] = jnp.where(trade, sc_far[0:2], sc[0:2]).astype(BF)
    grad_out[...] = jnp.where(trade, so_far[0:1], so[0:1]).astype(BF)
    links.finish()


def layer(*args):
    n = 220
    vm = pl.BlockSpec(memory_space=pltpu.VMEM)
    hbm = pl.BlockSpec(memory_space=pl.ANY)
    return pl.pallas_call(
        layer_kernel,
        out_shape=(
            jax.ShapeDtypeStruct((TOK, 256), BF),
            jax.ShapeDtypeStruct((D, 128), BF),
            jax.ShapeDtypeStruct((D, 128), BF),
            jax.ShapeDtypeStruct((2048, 256), BF),
            jax.ShapeDtypeStruct((2, 128), BF),
            jax.ShapeDtypeStruct((1, 256), BF),
        ),
        in_specs=[vm, vm, vm, hbm, hbm, hbm, vm, vm, vm, vm, vm],
        out_specs=[vm] * 6,
        scratch_shapes=[
            pltpu.VMEM((BLK, TOK), F32),
            pltpu.VMEM((TOK, TOK), F32),
            pltpu.VMEM((2048, 256), BF),
            pltpu.VMEM((2048, 256), BF),
            pltpu.VMEM((8, 128), F32),
            pltpu.VMEM((8, 128), F32),
            pltpu.VMEM((8, 256), F32),
            pltpu.VMEM((8, 256), F32),
            pltpu.VMEM((BLK, TOK, D), BF),
            pltpu.VMEM((D, 256), BF),
            pltpu.VMEM((BLK, TOK, 256), BF),
            pltpu.VMEM((BLK, BLK, TOK), F32),
            pltpu.VMEM((BLK, TOK), F32),
            pltpu.VMEM((BLK, TOK), F32),
            pltpu.VMEM((BLK, TOK), F32),
            pltpu.VMEM((ROWS, 256), BF),
            pltpu.VMEM((4, ROWS, 256), BF),
            pltpu.VMEM((4, 512, 256), BF),
            pltpu.VMEM((4, ROWS, 128), BF),
            pltpu.VMEM((3, ROWS, 128), BF),
            pltpu.VMEM((ROWS, 256), F32),
            pltpu.VMEM((ROWS, 128), BF),
            pltpu.VMEM((ROWS, 512), BF),
            pltpu.VMEM((4, 512, CROWS), BF),
            pltpu.VMEM((4, ROWS, 256), BF),
            pltpu.VMEM((3, ROWS, 256), BF),
            pltpu.VMEM((ROWS, 256), BF),
            pltpu.VMEM((BLK, CAP, 256), BF),
            pltpu.VMEM((4, 512, 256), BF),
            pltpu.VMEM((ROWS, 256), BF),
            pltpu.VMEM((ROWS, 256), BF),
            pltpu.VMEM((256, BLK * TOK), BF),
            pltpu.SemaphoreType.DMA((n,)),
            pltpu.SemaphoreType.DMA((n,)),
            pltpu.SemaphoreType.DMA((3,)),
        ],
        name="layer",
        compiler_params=pltpu.CompilerParams(collective_id=0, has_side_effects=True, vmem_limit_bytes=VMEM_LIMIT),
    )(*args)


def hand_over_kernel(*refs):
    count = len(refs) // 2
    sems = refs[-1]
    copies = [pltpu.make_async_copy(refs[i], refs[count + i], sems.at[i]) for i in range(count)]
    for copy in copies:
        copy.start()
    for copy in copies:
        copy.wait()


def hand_over(arrays):
    hbm = pl.BlockSpec(memory_space=pl.ANY)
    return pl.pallas_call(
        hand_over_kernel,
        out_shape=[jax.ShapeDtypeStruct(a.shape, a.dtype) for a in arrays],
        in_specs=[hbm] * len(arrays),
        out_specs=[hbm] * len(arrays),
        scratch_shapes=[pltpu.SemaphoreType.DMA((len(arrays),))],
        name="hand_over",
        compiler_params=pltpu.CompilerParams(vmem_limit_bytes=VMEM_LIMIT),
    )(*arrays)


def per_device(
    tokens, cotangent, routes, router_weight, w_gate, w_up, w_down,
    scale_gate, scale_up, scale_down, swapped,
):
    mixed, grad_gate, grad_up, grad_down, grad_in, grad_out = hand_over(layer(
        routes.T, router_weight.T, cotangent, tokens, w_gate[0], w_up[0], w_down[0],
        scale_gate, scale_up, scale_down, swapped[None],
    ))
    return mixed, grad_gate[None], grad_up[None], grad_down[None], grad_in[None], grad_out


def solution(mesh):
    in_specs = (
        P("expert", None),
        P("expert", "dp"),
        P("expert", None),
        P("expert", None),
        P("expert", None, "dp"),
        P("expert", None, "dp"),
        P("expert", None, "dp"),
        P("expert", "dp"),
        P("expert", "dp"),
        P("expert", "dp"),
        P(),
    )
    out_specs = (
        P("expert", "dp"),
        P("expert", None, "dp"),
        P("expert", None, "dp"),
        P("expert", None, "dp"),
        P("expert", None, "dp"),
        P("expert", "dp"),
    )
    return jax.shard_map(
        per_device, mesh=mesh, in_specs=in_specs, out_specs=out_specs, check_vma=False
    )
```

```python
import jax
import jax.numpy as jnp
from jax import lax
from jax.experimental import pallas as pl
from jax.experimental.pallas import tpu as pltpu
from jax.sharding import PartitionSpec as P

MESH = pl.DeviceIdType.MESH
BF = jnp.bfloat16
F32 = jnp.float32
CAP = 80
BLK = 16
TOK = 128
D = 4096
ROWS = BLK * CAP
CROWS = ROWS // 4
ORDER = (0, 1, 3, 2)
VMEM_LIMIT = 60 * 2**20
NT = (((1,), (1,)), ((), ()))
TN = (((0,), (0,)), ((), ()))


def place():
    dp = lax.axis_index("dp")
    ex = lax.axis_index("expert")
    y, zh = lax.div(dp, 4), lax.rem(dp, 4)
    x, zl, c = lax.div(ex, 4), lax.rem(lax.div(ex, 2), 2), lax.rem(ex, 2)
    return x, y, zh * 2 + zl, c


def device(x, y, z, c):
    x, y, z, c = lax.rem(x + 4, 4), lax.rem(y + 4, 4), lax.rem(z + 8, 8), lax.rem(c + 2, 2)
    return (y * 4 + lax.div(z, 2), slot(x, z, c))


def slot(x, z, c):
    return lax.rem(x + 4, 4) * 4 + lax.rem(z + 8, 2) * 2 + c


class Links:
    def __init__(self, send_sems, recv_sems, other):
        self.ss, self.rs, self.other = send_sems, recv_sems, other
        self.copies = []

    def send(self, src, dst, to):
        i = len(self.copies)
        copy = pltpu.make_async_remote_copy(
            src_ref=src,
            dst_ref=dst,
            send_sem=self.ss.at[i],
            recv_sem=self.rs.at[i],
            device_id=to,
            device_id_type=MESH,
        )
        copy.start()
        self.copies.append(copy)
        return i

    def arrived(self, i, dst):
        pltpu.make_async_remote_copy(
            src_ref=dst,
            dst_ref=dst,
            send_sem=self.ss.at[i],
            recv_sem=self.rs.at[i],
            device_id=self.other,
            device_id_type=MESH,
        ).wait_recv()

    def finish(self):
        for copy in self.copies:
            copy.wait_send()


def greet(devices):
    barrier = pltpu.get_barrier_semaphore()
    for to in devices:
        pl.semaphore_signal(barrier, inc=1, device_id=to, device_id_type=MESH)
    pl.semaphore_wait(barrier, len(devices))


def layer_kernel(
    routes, weights, cot, tok, wg, wu, wd, sg, su, sd, swapped,
    mixed, grad_gate, grad_up, grad_down, grad_in, grad_out,
    comb, comb_t, own_gd, far_gd, sc, sc_far, so, so_far,
    toks, w_in, cots, combs, cw_own, cw_par, pos, rg, di4, wd4, part, rz,
    pre, hid, hz, hz_t, op, ro, eo, ret, gd, gi, gi_far, spread_t, ss, rs, local,
):
    x, y, z, c = place()
    zl = lax.rem(z, 2)
    zh = lax.div(z, 2)
    me = slot(x, z, c)
    inner = lax.rem(me, 4)
    dp = lax.axis_index("dp")
    sibling = device(x, y, z, 1 - c)
    far = device(x + 2, y, z, c)
    up, down = device(x, y, z + 1, c), device(x, y, z - 1, c)
    chip = x * 2 + zl
    links = Links(ss, rs, sibling)

    def chip_at(k):
        q = lax.rem(chip + k + 8, 8)
        return lax.div(q, 2), zh * 2 + lax.rem(q, 2)

    def columns(j):
        return pl.ds(pl.multiple_of(j * 128, 128), 128)

    def quarter(j):
        return pl.ds(pl.multiple_of(j * 512, 512), 512)

    def chunk(j):
        return pl.ds(pl.multiple_of(j * CROWS, CROWS), CROWS)

    def block(r):
        return pl.ds(pl.multiple_of(r * CAP, CAP), CAP)

    loads = [
        pltpu.make_async_copy(tok, toks.at[me], local.at[0]),
        pltpu.make_async_copy(wg, w_in.at[:, pl.ds(0, 128)], local.at[1]),
        pltpu.make_async_copy(wu, w_in.at[:, pl.ds(128, 128)], local.at[2]),
    ]
    for load in loads:
        load.start()

    names = lax.broadcasted_iota(jnp.int32, (TOK, TOK), 0)
    dense = jnp.zeros((TOK, TOK), F32)
    for k in range(routes.shape[0]):
        dense += jnp.where(routes[k:k + 1, :] == names, weights[k:k + 1, :], 0.0)
    comb[...] = dense[0:BLK]
    comb_t[...] = dense.T

    peers = [(dp, lax.rem(me + k, 16)) for k in range(1, 16)]
    peers.append(device(x, y, z - 1 + 2 * zl, c))
    for d in range(1, 4):
        peers.append(device(x, y + d, z, c))
        peers.append(device(x, y, z + 2 * d, c))
        peers.append(device(x + 2, y + d, z, c))
    greet(peers)

    first = []
    for k in range(1, 8):
        qx, qz = chip_at(k)
        to = device(qx, y, qz, c)
        first.append((k, links.send(comb, combs.at[me], to), links.send(cot, cots.at[me], to)))
    over = [(0, links.send(comb, combs.at[me], sibling), links.send(cot, cots.at[me], sibling))]
    wd_ids = []
    for d in (1, 3, 2):
        wd_ids.append((d, links.send(wd.at[quarter(lax.rem(y + d, 4))], wd4.at[y], device(x, y + d, z, c))))

    lower, upper = pl.ds(0, 64), pl.ds(64, 64)
    halves = {"l": lower, "u": upper}
    pair = {}

    def to_sibling(d, dz, rows):
        s = slot(x - d, z + dz, c)
        pair.setdefault((d, dz), []).append((links.send(toks.at[s, rows], toks.at[s, rows], sibling), rows))

    z_ids, x_ids, f_ids = {}, {}, {}
    z_ids["l"] = links.send(tok.at[lower], toks.at[me, lower], up)
    z_ids["u"] = links.send(tok.at[upper], toks.at[me, upper], down)
    for d, h in ((1, "l"), (3, "u"), (1, "u"), (3, "l")):
        x_ids[d, 0, h] = links.send(tok.at[halves[h]], toks.at[me, halves[h]], device(x + d, y, z, c))
    pair[0, 0] = [(links.send(tok, toks.at[me], sibling), pl.ds(0, TOK))]

    combs[me] = comb[...]
    cots[me] = cot[...]
    wd4[y] = wd[quarter(y), :]
    for k, ia, ib in first:
        qx, qz = chip_at(-k)
        s = slot(qx, qz, c)
        links.arrived(ia, combs.at[s])
        links.arrived(ib, cots.at[s])
        over.append((k, links.send(combs.at[s], combs.at[s], sibling), links.send(cots.at[s], cots.at[s], sibling)))
    for k, ia, ib in over:
        qx, qz = chip_at(-k)
        s = slot(qx, qz, 1 - c)
        links.arrived(ia, combs.at[s])
        links.arrived(ib, cots.at[s])

    experts = lax.broadcasted_iota(jnp.int32, (BLK, BLK, TOK), 1)
    table = combs[...]
    cw = jnp.sum(jnp.where(experts == me, table, 0.0), axis=1)
    cw_own[...] = cw
    cw_par[...] = jnp.sum(jnp.where(experts == lax.rem(me + 8, 16), table, 0.0), axis=1)
    before = (
        lax.broadcasted_iota(jnp.int32, (TOK, TOK), 0) < lax.broadcasted_iota(jnp.int32, (TOK, TOK), 1)
    ).astype(F32).astype(BF)
    pos[...] = jnp.dot((cw > 0).astype(BF), before, preferred_element_type=F32)
    spots = lax.broadcasted_iota(jnp.int32, (CAP, TOK), 0).astype(F32)
    down_scale = sd[...].astype(F32)

    def compact(r, _):
        weight = cw_own[pl.ds(r, 1), :]
        hit = (pos[pl.ds(r, 1), :] == spots) & (weight > 0)
        picked = jnp.dot(jnp.where(hit, 1.0, 0.0).astype(BF), cots[r], preferred_element_type=F32)
        w = jnp.sum(jnp.where(hit, weight, 0.0), axis=1, keepdims=True)
        routed = (picked * w).astype(BF)
        rg[block(r), :] = routed
        di4[y, block(r), :] = (routed.astype(F32) * down_scale).astype(BF)
        return 0

    def rows_of(d, part=None):
        start = lax.rem(x - d + 4, 4) * CROWS
        if part is None:
            return pl.ds(pl.multiple_of(start, CROWS), CROWS)
        return pl.ds(pl.multiple_of(start + part * (CROWS // 2), CROWS // 2), CROWS // 2)

    y_ids = {}
    for g in ORDER:
        at = lax.rem(x - g + 4, 4) * 4
        lax.fori_loop(at, at + 4, compact, 0)
        rows = rows_of(g)
        for d in (1, 3):
            y_ids[g, d] = links.send(di4.at[y, rows], di4.at[y, rows], device(x, y + d, z, c))
    for d, i in wd_ids:
        links.arrived(i, wd4.at[lax.rem(y - d + 4, 4)])

    def y_fwd(g):
        for d, h in ((1, 0), (3, 1)):
            j = lax.rem(y - d + 4, 4)
            links.arrived(y_ids[g, d], di4.at[j, rows_of(g)])
            rows = rows_of(g, h)
            y_ids[g, d, "f"] = links.send(di4.at[j, rows], di4.at[j, rows], device(x, y + d, z, c))

    zr = {}

    def terms(g):
        rows = rows_of(g)
        for d, h in ((1, 0), (3, 1)):
            links.arrived(y_ids[g, d, "f"], di4.at[lax.rem(y + 2, 4), rows_of(g, h)])
        acc = lax.dot_general(di4[0, rows, :], wd4[0], NT, preferred_element_type=F32)
        for j in range(1, 4):
            acc += lax.dot_general(di4[j, rows, :], wd4[j], NT, preferred_element_type=F32)
        acc = acc.astype(BF)
        for j in range(4):
            part[j, rows, :] = acc[:, j * 128:(j + 1) * 128]
        for d in (2, 1, 3):
            zr[g, d] = links.send(part.at[lax.rem(zh + d, 4), rows], rz.at[d - 1, rows], device(x, y, z + 2 * d, c))

    def z_own():
        s = slot(x, z + 1, c)
        for h, order in (("l", (1, 3)), ("u", (3, 1))):
            rows = halves[h]
            links.arrived(z_ids[h], toks.at[s, rows])
            for d in order:
                x_ids[d, 1, h] = links.send(toks.at[s, rows], toks.at[s, rows], device(x + d, y, z, c))
            to_sibling(0, 1, rows)

    def x_first(dz):
        for d, h in ((1, "l"), (3, "u")):
            s = slot(x - d, z + dz, c)
            rows = halves[h]
            links.arrived(x_ids[d, dz, h], toks.at[s, rows])
            f_ids[d, dz] = links.send(toks.at[s, rows], toks.at[s, rows], device(x + d, y, z, c))
            to_sibling(d, dz, rows)

    def x_second(dz):
        for d, h in ((1, "u"), (3, "l")):
            s = slot(x - d, z + dz, c)
            links.arrived(x_ids[d, dz, h], toks.at[s, halves[h]])
            to_sibling(d, dz, halves[h])

    def x_far(dz):
        for d, h in ((1, "l"), (3, "u")):
            s = slot(x + 2, z + dz, c)
            links.arrived(f_ids[d, dz], toks.at[s, halves[h]])
            to_sibling(2, dz, halves[h])

    gate_scale = sg[...].astype(F32)
    up_scale = su[...].astype(F32)
    hid_ids = {}

    def group(d):
        gx = lax.rem(x - d + 4, 4)
        for dz in (0, 1):
            s = slot(x - d, z + dz, 1 - c)
            for i, rows in pair[d, dz]:
                links.arrived(i, toks.at[s, rows])

        def deepen(k, acc):
            at = pl.ds(pl.multiple_of(k * 1024, 1024), 1024)
            left = toks[pl.ds(gx * 4, 4), :, at].reshape(4 * TOK, 1024)
            return acc + jnp.dot(left, w_in[at, :], preferred_element_type=F32)

        acc = lax.fori_loop(0, 4, deepen, jnp.zeros((4 * TOK, 256), F32))
        for j in range(4):
            r = gx * 4 + j
            hit = (pos[pl.ds(r, 1), :] == spots) & (cw_own[pl.ds(r, 1), :] > 0)
            pre[block(r), :] = jnp.dot(
                jnp.where(hit, 1.0, 0.0), acc[j * TOK:(j + 1) * TOK], precision=lax.Precision.HIGHEST,
                preferred_element_type=F32,
            )
        rows = chunk(gx)
        gate_act = pre[rows, 0:128] * gate_scale
        up_act = pre[rows, 128:256] * up_scale
        hid[rows, :] = (gate_act * jax.nn.sigmoid(gate_act) * up_act).astype(BF)
        hz[rows, columns(zh)] = hid[rows, :]
        for dz in (1, 3):
            hid_ids[d, dz] = links.send(hid.at[rows], hz.at[rows, columns(zh)], device(x, y, z + 2 * dz, c))

    def hid_fwd(d):
        for dz, h in ((1, 0), (3, 1)):
            at = columns(lax.rem(zh - dz + 4, 4))
            links.arrived(hid_ids[d, dz], hz.at[rows_of(d), at])
            rows = rows_of(d, h)
            hid_ids[d, dz, "f"] = links.send(hz.at[rows, at], hz.at[rows, at], device(x, y, z + 2 * dz, c))

    out_ids = {}

    def project(d):
        rows = chunk(lax.rem(x - d + 4, 4))
        for dz, h in ((1, 0), (3, 1)):
            links.arrived(hid_ids[d, dz, "f"], hz.at[rows_of(d, h), columns(lax.rem(zh + 2, 4))])
        left = hz[rows, :]
        hz_t[lax.rem(x - d + 4, 4)] = left.T
        for dy in (2, 1, 3, 0):
            j = lax.rem(y + dy, 4)
            op[j, rows, :] = jnp.dot(left, wd4[j], preferred_element_type=F32).astype(BF)
            if dy:
                out_ids[d, dy] = links.send(op.at[j, rows], ro.at[dy - 1, rows], device(x, y + dy, z, c))

    so[...] = jnp.zeros_like(so)
    back = {}

    def give(d):
        gx = lax.rem(x - d + 4, 4)
        rows = chunk(gx)
        for dy in (1, 3, 2):
            links.arrived(out_ids[d, dy], ro.at[dy - 1, rows])
        total = op[y, rows, :].astype(F32)
        for dy in (1, 2, 3):
            total += ro[dy - 1, rows, :].astype(F32)
        so[0:1, :] += jnp.sum(total * rg[rows, :].astype(F32), axis=0, keepdims=True)
        eo[rows, :] = (total * down_scale).astype(BF)
        for j in range(4):
            r = gx * 4 + lax.rem(inner + j, 4)
            if d == 0 and j == 0:
                ret[me] = eo[block(r), :]
            else:
                back[d, j] = links.send(eo.at[block(r)], ret.at[me], (dp, r))

    sc[...] = jnp.zeros_like(sc)
    gi_ids = {}

    def gradient(g):
        rows = rows_of(g)
        for d in (1, 2, 3):
            links.arrived(zr[g, d], rz.at[d - 1, rows])
        total = part[zh, rows, :].astype(F32)
        for d in (1, 2, 3):
            total += rz[d - 1, rows, :].astype(F32)
        gate_pre, up_pre = pre[rows, 0:128], pre[rows, 128:256]
        gate_act, up_act = gate_pre * gate_scale, up_pre * up_scale
        sig = jax.nn.sigmoid(gate_act)
        gate_grad = total * up_act * sig * (1.0 + gate_act * (1.0 - sig))
        up_grad = total * (gate_act * sig)
        sc[0:1, :] += jnp.sum(gate_grad * gate_pre, axis=0, keepdims=True)
        sc[1:2, :] += jnp.sum(up_grad * up_pre, axis=0, keepdims=True)
        gi[rows, 0:128] = (gate_grad * gate_scale).astype(BF)
        gi[rows, 128:256] = (up_grad * up_scale).astype(BF)

    def trade_gi(g):
        gi_ids[g] = links.send(gi.at[rows_of(g)], gi_far.at[rows_of(g)], far)

    for load in loads:
        load.wait()
    z_own()
    y_fwd(0)
    group(0)
    x_first(0)
    y_fwd(1)
    terms(0)
    y_fwd(3)
    x_second(0)
    terms(1)
    hid_fwd(0)
    y_fwd(2)
    x_first(1)
    terms(3)
    terms(2)
    project(0)
    x_second(1)
    x_far(0)
    group(1)
    group(3)
    x_far(1)
    hid_fwd(1)
    hid_fwd(3)
    group(2)
    gradient(0)
    gradient(1)
    gradient(3)
    for g in (0, 1, 3):
        trade_gi(g)
    project(1)
    project(3)
    hid_fwd(2)
    gradient(2)
    trade_gi(2)
    project(2)

    gd_ids = {}
    for d in (2, 1, 3, 0):
        j = lax.rem(y + d, 4)
        acc = jnp.dot(hz_t[0], di4[j, 0:CROWS, :], preferred_element_type=F32)
        for i in range(1, 4):
            acc += jnp.dot(hz_t[i], di4[j, i * CROWS:(i + 1) * CROWS, :], preferred_element_type=F32)
        gd[j] = acc.astype(BF)
        gd_ids["far", d] = links.send(gd.at[j], far_gd.at[quarter(y)], device(x + 2, y + d, z, c))
        if d:
            gd_ids["own", d] = links.send(gd.at[j], own_gd.at[quarter(y)], device(x, y + d, z, c))
        else:
            own_gd[quarter(y), :] = gd[j]
    give(0)
    give(1)
    sc_id = links.send(sc, sc_far, far)
    give(3)
    give(2)
    so_id = links.send(so, so_far, far)

    for g in ORDER:
        links.arrived(gi_ids[g], gi_far.at[rows_of((g + 2) % 4)])
    trade = jnp.sum(jnp.where(lax.broadcasted_iota(jnp.int32, (1, BLK), 1) == me, swapped[...], 0), axis=1, keepdims=True) > 0
    cw_sel = jnp.where(trade, cw_par[...], cw_own[...])
    cw_par[...] = cw_sel
    pos[...] = jnp.dot((cw_sel > 0).astype(BF), before, preferred_element_type=F32)

    def expand(r, _):
        hit = (pos[pl.ds(r, 1), :] == spots) & (cw_par[pl.ds(r, 1), :] > 0)
        chosen = jnp.where(trade, gi_far[block(r), :].astype(F32), gi[block(r), :].astype(F32)).astype(BF)
        spread_t[:, columns(r)] = lax.dot_general(
            chosen, jnp.where(hit, 1.0, 0.0).astype(BF), TN, preferred_element_type=F32
        ).astype(BF)
        return 0

    lax.fori_loop(0, BLK, expand, 0)

    def weight_grad(k, _):
        at = pl.ds(pl.multiple_of(k * 512, 512), 512)
        right = toks[:, :, at].reshape(BLK * TOK, 512)
        grad = jnp.dot(spread_t[...], right, preferred_element_type=F32).astype(BF).T
        grad_gate[at, :] = grad[:, 0:128]
        grad_up[at, :] = grad[:, 128:256]
        return 0

    lax.fori_loop(0, D // 512, weight_grad, 0)

    for (d, j), k in back.items():
        links.arrived(k, ret.at[lax.rem(x + d, 4) * 4 + lax.rem(inner + 4 - j, 4)])
    places = jnp.dot((comb[...] > 0).astype(BF), before, preferred_element_type=F32)
    total = jnp.zeros((TOK, 256), F32)
    for e in range(BLK):
        hit = (places[e:e + 1, :] == spots) & (comb[e:e + 1, :] > 0)
        total += (
            lax.dot_general(jnp.where(hit, 1.0, 0.0).astype(BF), ret[e], TN, preferred_element_type=F32)
            * comb_t[:, e:e + 1]
        )
    mixed[...] = total.astype(BF)
    links.arrived(sc_id, sc_far)
    links.arrived(so_id, so_far)
    for d in (1, 2, 3, 0):
        rows = quarter(lax.rem(y - d + 4, 4))
        links.arrived(gd_ids["far", d], far_gd.at[rows])
        if d:
            links.arrived(gd_ids["own", d], own_gd.at[rows])
    grad_down[...] = jnp.where(trade, far_gd[...], own_gd[...])
    grad_in[...] = jnp.where(trade, sc_far[0:2], sc[0:2]).astype(BF)
    grad_out[...] = jnp.where(trade, so_far[0:1], so[0:1]).astype(BF)
    links.finish()


def layer(*args):
    n = 160
    vm = pl.BlockSpec(memory_space=pltpu.VMEM)
    hbm = pl.BlockSpec(memory_space=pl.ANY)
    return pl.pallas_call(
        layer_kernel,
        out_shape=(
            jax.ShapeDtypeStruct((TOK, 256), BF),
            jax.ShapeDtypeStruct((D, 128), BF),
            jax.ShapeDtypeStruct((D, 128), BF),
            jax.ShapeDtypeStruct((2048, 256), BF),
            jax.ShapeDtypeStruct((2, 128), BF),
            jax.ShapeDtypeStruct((1, 256), BF),
        ),
        in_specs=[vm, vm, vm, hbm, hbm, hbm, vm, vm, vm, vm, vm],
        out_specs=[vm] * 6,
        scratch_shapes=[
            pltpu.VMEM((BLK, TOK), F32),
            pltpu.VMEM((TOK, TOK), F32),
            pltpu.VMEM((2048, 256), BF),
            pltpu.VMEM((2048, 256), BF),
            pltpu.VMEM((8, 128), F32),
            pltpu.VMEM((8, 128), F32),
            pltpu.VMEM((8, 256), F32),
            pltpu.VMEM((8, 256), F32),
            pltpu.VMEM((BLK, TOK, D), BF),
            pltpu.VMEM((D, 256), BF),
            pltpu.VMEM((BLK, TOK, 256), BF),
            pltpu.VMEM((BLK, BLK, TOK), F32),
            pltpu.VMEM((BLK, TOK), F32),
            pltpu.VMEM((BLK, TOK), F32),
            pltpu.VMEM((BLK, TOK), F32),
            pltpu.VMEM((ROWS, 256), BF),
            pltpu.VMEM((4, ROWS, 256), BF),
            pltpu.VMEM((4, 512, 256), BF),
            pltpu.VMEM((4, ROWS, 128), BF),
            pltpu.VMEM((3, ROWS, 128), BF),
            pltpu.VMEM((ROWS, 256), F32),
            pltpu.VMEM((ROWS, 128), BF),
            pltpu.VMEM((ROWS, 512), BF),
            pltpu.VMEM((4, 512, CROWS), BF),
            pltpu.VMEM((4, ROWS, 256), BF),
            pltpu.VMEM((3, ROWS, 256), BF),
            pltpu.VMEM((ROWS, 256), BF),
            pltpu.VMEM((BLK, CAP, 256), BF),
            pltpu.VMEM((4, 512, 256), BF),
            pltpu.VMEM((ROWS, 256), BF),
            pltpu.VMEM((ROWS, 256), BF),
            pltpu.VMEM((256, BLK * TOK), BF),
            pltpu.SemaphoreType.DMA((n,)),
            pltpu.SemaphoreType.DMA((n,)),
            pltpu.SemaphoreType.DMA((3,)),
        ],
        name="layer",
        compiler_params=pltpu.CompilerParams(collective_id=0, has_side_effects=True, vmem_limit_bytes=VMEM_LIMIT),
    )(*args)


def hand_over_kernel(*refs):
    count = (len(refs) - 2) // 3
    given, out, held = refs[:count], refs[count:2 * count], refs[2 * count:3 * count]
    loads = [pltpu.make_async_copy(given[i], held[i], refs[-2].at[i]) for i in range(count)]
    stores = [pltpu.make_async_copy(held[i], out[i], refs[-1].at[i]) for i in range(count)]
    for load in loads:
        load.start()
    for load, store in zip(loads, stores):
        load.wait()
        store.start()
    for store in stores:
        store.wait()


def hand_over(arrays):
    hbm = pl.BlockSpec(memory_space=pl.ANY)
    return pl.pallas_call(
        hand_over_kernel,
        out_shape=[jax.ShapeDtypeStruct(a.shape, a.dtype) for a in arrays],
        in_specs=[hbm] * len(arrays),
        out_specs=[hbm] * len(arrays),
        scratch_shapes=[pltpu.VMEM(a.shape, a.dtype) for a in arrays]
        + [pltpu.SemaphoreType.DMA((len(arrays),))] * 2,
        name="hand_over",
        compiler_params=pltpu.CompilerParams(vmem_limit_bytes=VMEM_LIMIT),
    )(*arrays)


def per_device(
    tokens, cotangent, routes, router_weight, w_gate, w_up, w_down,
    scale_gate, scale_up, scale_down, swapped,
):
    mixed, grad_gate, grad_up, grad_down, grad_in, grad_out = hand_over(layer(
        routes.T, router_weight.T, cotangent, tokens, w_gate[0], w_up[0], w_down[0],
        scale_gate, scale_up, scale_down, swapped[None],
    ))
    return mixed, grad_gate[None], grad_up[None], grad_down[None], grad_in[None], grad_out


def solution(mesh):
    in_specs = (
        P("expert", None),
        P("expert", "dp"),
        P("expert", None),
        P("expert", None),
        P("expert", None, "dp"),
        P("expert", None, "dp"),
        P("expert", None, "dp"),
        P("expert", "dp"),
        P("expert", "dp"),
        P("expert", "dp"),
        P(),
    )
    out_specs = (
        P("expert", "dp"),
        P("expert", None, "dp"),
        P("expert", None, "dp"),
        P("expert", None, "dp"),
        P("expert", None, "dp"),
        P("expert", "dp"),
    )
    return jax.shard_map(
        per_device, mesh=mesh, in_specs=in_specs, out_specs=out_specs, check_vma=False
    )
```

```python
import jax
import jax.numpy as jnp
from jax import lax
from jax.experimental import pallas as pl
from jax.experimental.pallas import tpu as pltpu
from jax.sharding import PartitionSpec as P

MESH = pl.DeviceIdType.MESH
BF = jnp.bfloat16
F32 = jnp.float32
CAP = 80
BLK = 16
TOK = 128
D = 4096
ROWS = BLK * CAP
CROWS = ROWS // 4
ORDER = (0, 1, 3, 2)
VMEM_LIMIT = 60 * 2**20
NT = (((1,), (1,)), ((), ()))
TN = (((0,), (0,)), ((), ()))


def place():
    dp = lax.axis_index("dp")
    ex = lax.axis_index("expert")
    y, zh = lax.div(dp, 4), lax.rem(dp, 4)
    x, zl, c = lax.div(ex, 4), lax.rem(lax.div(ex, 2), 2), lax.rem(ex, 2)
    return x, y, zh * 2 + zl, c


def device(x, y, z, c):
    x, y, z, c = lax.rem(x + 4, 4), lax.rem(y + 4, 4), lax.rem(z + 8, 8), lax.rem(c + 2, 2)
    return (y * 4 + lax.div(z, 2), slot(x, z, c))


def slot(x, z, c):
    return lax.rem(x + 4, 4) * 4 + lax.rem(z + 8, 2) * 2 + c


class Links:
    def __init__(self, send_sems, recv_sems, other):
        self.ss, self.rs, self.other = send_sems, recv_sems, other
        self.copies = []

    def send(self, src, dst, to):
        i = len(self.copies)
        copy = pltpu.make_async_remote_copy(
            src_ref=src,
            dst_ref=dst,
            send_sem=self.ss.at[i],
            recv_sem=self.rs.at[i],
            device_id=to,
            device_id_type=MESH,
        )
        copy.start()
        self.copies.append(copy)
        return i

    def arrived(self, i, dst):
        pltpu.make_async_remote_copy(
            src_ref=dst,
            dst_ref=dst,
            send_sem=self.ss.at[i],
            recv_sem=self.rs.at[i],
            device_id=self.other,
            device_id_type=MESH,
        ).wait_recv()

    def finish(self):
        for copy in self.copies:
            copy.wait_send()


def greet(devices):
    barrier = pltpu.get_barrier_semaphore()
    for to in devices:
        pl.semaphore_signal(barrier, inc=1, device_id=to, device_id_type=MESH)
    pl.semaphore_wait(barrier, len(devices))


def layer_kernel(
    routes, weights, cot, tok, wg, wu, wd, sg, su, sd, swapped,
    mixed, grad_gate, grad_up, grad_down, grad_in, grad_out,
    comb, comb_t, own_gd, far_gd, sc, sc_far, so, so_far,
    toks, w_in, cots, combs, cw_own, cw_par, pos, rg, di4, wd4, part, rz,
    pre, hid, hz, hz_t, op, ro, eo, ret, gd, gi, gi_far, spread_t, ss, rs, local,
):
    x, y, z, c = place()
    zl = lax.rem(z, 2)
    zh = lax.div(z, 2)
    me = slot(x, z, c)
    inner = lax.rem(me, 4)
    dp = lax.axis_index("dp")
    sibling = device(x, y, z, 1 - c)
    far = device(x + 2, y, z, c)
    up, down = device(x, y, z + 1, c), device(x, y, z - 1, c)
    chip = x * 2 + zl
    links = Links(ss, rs, sibling)

    def chip_at(k):
        q = lax.rem(chip + k + 8, 8)
        return lax.div(q, 2), zh * 2 + lax.rem(q, 2)

    def columns(j):
        return pl.ds(pl.multiple_of(j * 128, 128), 128)

    def quarter(j):
        return pl.ds(pl.multiple_of(j * 512, 512), 512)

    def chunk(j):
        return pl.ds(pl.multiple_of(j * CROWS, CROWS), CROWS)

    def block(r):
        return pl.ds(pl.multiple_of(r * CAP, CAP), CAP)

    loads = [
        pltpu.make_async_copy(tok, toks.at[me], local.at[0]),
        pltpu.make_async_copy(wg, w_in.at[:, pl.ds(0, 128)], local.at[1]),
        pltpu.make_async_copy(wu, w_in.at[:, pl.ds(128, 128)], local.at[2]),
    ]
    for load in loads:
        load.start()

    names = lax.broadcasted_iota(jnp.int32, (TOK, TOK), 0)
    dense = jnp.zeros((TOK, TOK), F32)
    for k in range(routes.shape[0]):
        dense += jnp.where(routes[k:k + 1, :] == names, weights[k:k + 1, :], 0.0)
    comb[...] = dense[0:BLK]
    comb_t[...] = dense.T

    peers = [(dp, lax.rem(me + k, 16)) for k in range(1, 16)]
    peers.append(device(x, y, z - 1 + 2 * zl, c))
    for d in range(1, 4):
        peers.append(device(x, y + d, z, c))
        peers.append(device(x, y, z + 2 * d, c))
        peers.append(device(x + 2, y + d, z, c))
    greet(peers)

    first = []
    for k in range(1, 8):
        qx, qz = chip_at(k)
        to = device(qx, y, qz, c)
        first.append((k, links.send(comb, combs.at[me], to), links.send(cot, cots.at[me], to)))
    over = [(0, links.send(comb, combs.at[me], sibling), links.send(cot, cots.at[me], sibling))]
    wd_ids = []
    for d in (1, 3, 2):
        wd_ids.append((d, links.send(wd.at[quarter(lax.rem(y + d, 4))], wd4.at[y], device(x, y + d, z, c))))

    lower, upper = pl.ds(0, 64), pl.ds(64, 64)
    halves = {"l": lower, "u": upper}
    pair = {}

    def to_sibling(d, dz, rows):
        s = slot(x - d, z + dz, c)
        pair.setdefault((d, dz), []).append((links.send(toks.at[s, rows], toks.at[s, rows], sibling), rows))

    z_ids, x_ids, f_ids = {}, {}, {}
    z_ids["l"] = links.send(tok.at[lower], toks.at[me, lower], up)
    z_ids["u"] = links.send(tok.at[upper], toks.at[me, upper], down)
    for d, h in ((1, "l"), (3, "u")):
        x_ids[d, 0, h] = links.send(tok.at[halves[h]], toks.at[me, halves[h]], device(x + d, y, z, c))
    pair[0, 0] = [(links.send(tok, toks.at[me], sibling), pl.ds(0, TOK))]

    def z_own():
        s = slot(x, z + 1, c)
        for h, order in (("l", (1, 3)), ("u", (3, 1))):
            rows = halves[h]
            links.arrived(z_ids[h], toks.at[s, rows])
            for d in order:
                x_ids[d, 1, h] = links.send(toks.at[s, rows], toks.at[s, rows], device(x + d, y, z, c))
            to_sibling(0, 1, rows)

    def x_first(dz):
        for d, h in ((1, "l"), (3, "u")):
            s = slot(x - d, z + dz, c)
            rows = halves[h]
            links.arrived(x_ids[d, dz, h], toks.at[s, rows])
            f_ids[d, dz] = links.send(toks.at[s, rows], toks.at[s, rows], device(x + d, y, z, c))
            to_sibling(d, dz, rows)

    def x_second(dz):
        for d, h in ((1, "u"), (3, "l")):
            s = slot(x - d, z + dz, c)
            links.arrived(x_ids[d, dz, h], toks.at[s, halves[h]])
            to_sibling(d, dz, halves[h])

    def x_far(dz):
        for d, h in ((1, "l"), (3, "u")):
            s = slot(x + 2, z + dz, c)
            links.arrived(f_ids[d, dz], toks.at[s, halves[h]])
            to_sibling(2, dz, halves[h])

    combs[me] = comb[...]
    cots[me] = cot[...]
    wd4[y] = wd[quarter(y), :]
    for k, ia, ib in first:
        qx, qz = chip_at(-k)
        s = slot(qx, qz, c)
        links.arrived(ia, combs.at[s])
        links.arrived(ib, cots.at[s])
        over.append((k, links.send(combs.at[s], combs.at[s], sibling), links.send(cots.at[s], cots.at[s], sibling)))
    for d, h in ((1, "u"), (3, "l")):
        x_ids[d, 0, h] = links.send(tok.at[halves[h]], toks.at[me, halves[h]], device(x + d, y, z, c))
    z_own()
    for k, ia, ib in over:
        qx, qz = chip_at(-k)
        s = slot(qx, qz, 1 - c)
        links.arrived(ia, combs.at[s])
        links.arrived(ib, cots.at[s])

    experts = lax.broadcasted_iota(jnp.int32, (BLK, BLK, TOK), 1)
    table = combs[...]
    cw = jnp.sum(jnp.where(experts == me, table, 0.0), axis=1)
    cw_own[...] = cw
    cw_par[...] = jnp.sum(jnp.where(experts == lax.rem(me + 8, 16), table, 0.0), axis=1)
    before = (
        lax.broadcasted_iota(jnp.int32, (TOK, TOK), 0) < lax.broadcasted_iota(jnp.int32, (TOK, TOK), 1)
    ).astype(F32).astype(BF)
    pos[...] = jnp.dot((cw > 0).astype(BF), before, preferred_element_type=F32)
    spots = lax.broadcasted_iota(jnp.int32, (CAP, TOK), 0).astype(F32)
    down_scale = sd[...].astype(F32)

    def compact(r, _):
        weight = cw_own[pl.ds(r, 1), :]
        hit = (pos[pl.ds(r, 1), :] == spots) & (weight > 0)
        picked = jnp.dot(jnp.where(hit, 1.0, 0.0).astype(BF), cots[r], preferred_element_type=F32)
        w = jnp.sum(jnp.where(hit, weight, 0.0), axis=1, keepdims=True)
        routed = (picked * w).astype(BF)
        rg[block(r), :] = routed
        di4[y, block(r), :] = (routed.astype(F32) * down_scale).astype(BF)
        return 0

    def rows_of(d, part=None):
        start = lax.rem(x - d + 4, 4) * CROWS
        if part is None:
            return pl.ds(pl.multiple_of(start, CROWS), CROWS)
        return pl.ds(pl.multiple_of(start + part * (CROWS // 2), CROWS // 2), CROWS // 2)

    y_ids = {}
    for g in ORDER:
        at = lax.rem(x - g + 4, 4) * 4
        lax.fori_loop(at, at + 4, compact, 0)
        rows = rows_of(g)
        for d in (1, 3):
            y_ids[g, d] = links.send(di4.at[y, rows], di4.at[y, rows], device(x, y + d, z, c))
    for d, i in wd_ids:
        links.arrived(i, wd4.at[lax.rem(y - d + 4, 4)])

    def y_fwd(g):
        for d, h in ((1, 0), (3, 1)):
            j = lax.rem(y - d + 4, 4)
            links.arrived(y_ids[g, d], di4.at[j, rows_of(g)])
            rows = rows_of(g, h)
            y_ids[g, d, "f"] = links.send(di4.at[j, rows], di4.at[j, rows], device(x, y + d, z, c))

    zr = {}

    def terms(g):
        rows = rows_of(g)
        for d, h in ((1, 0), (3, 1)):
            links.arrived(y_ids[g, d, "f"], di4.at[lax.rem(y + 2, 4), rows_of(g, h)])
        acc = lax.dot_general(di4[0, rows, :], wd4[0], NT, preferred_element_type=F32)
        for j in range(1, 4):
            acc += lax.dot_general(di4[j, rows, :], wd4[j], NT, preferred_element_type=F32)
        acc = acc.astype(BF)
        for j in range(4):
            part[j, rows, :] = acc[:, j * 128:(j + 1) * 128]
        for d in (2, 1, 3):
            zr[g, d] = links.send(part.at[lax.rem(zh + d, 4), rows], rz.at[d - 1, rows], device(x, y, z + 2 * d, c))

    gate_scale = sg[...].astype(F32)
    up_scale = su[...].astype(F32)
    hid_ids = {}

    def group(d):
        gx = lax.rem(x - d + 4, 4)
        for dz in (0, 1):
            s = slot(x - d, z + dz, 1 - c)
            for i, rows in pair[d, dz]:
                links.arrived(i, toks.at[s, rows])

        def deepen(k, acc):
            at = pl.ds(pl.multiple_of(k * 1024, 1024), 1024)
            left = toks[pl.ds(gx * 4, 4), :, at].reshape(4 * TOK, 1024)
            return acc + jnp.dot(left, w_in[at, :], preferred_element_type=F32)

        acc = lax.fori_loop(0, 4, deepen, jnp.zeros((4 * TOK, 256), F32))
        for j in range(4):
            r = gx * 4 + j
            hit = (pos[pl.ds(r, 1), :] == spots) & (cw_own[pl.ds(r, 1), :] > 0)
            pre[block(r), :] = jnp.dot(
                jnp.where(hit, 1.0, 0.0), acc[j * TOK:(j + 1) * TOK], precision=lax.Precision.HIGHEST,
                preferred_element_type=F32,
            )
        rows = chunk(gx)
        gate_act = pre[rows, 0:128] * gate_scale
        up_act = pre[rows, 128:256] * up_scale
        hid[rows, :] = (gate_act * jax.nn.sigmoid(gate_act) * up_act).astype(BF)
        hz[rows, columns(zh)] = hid[rows, :]
        for dz in (1, 3):
            hid_ids[d, dz] = links.send(hid.at[rows], hz.at[rows, columns(zh)], device(x, y, z + 2 * dz, c))

    def hid_fwd(d):
        for dz, h in ((1, 0), (3, 1)):
            at = columns(lax.rem(zh - dz + 4, 4))
            links.arrived(hid_ids[d, dz], hz.at[rows_of(d), at])
            rows = rows_of(d, h)
            hid_ids[d, dz, "f"] = links.send(hz.at[rows, at], hz.at[rows, at], device(x, y, z + 2 * dz, c))

    out_ids = {}

    def project(d):
        rows = chunk(lax.rem(x - d + 4, 4))
        for dz, h in ((1, 0), (3, 1)):
            links.arrived(hid_ids[d, dz, "f"], hz.at[rows_of(d, h), columns(lax.rem(zh + 2, 4))])
        left = hz[rows, :]
        hz_t[lax.rem(x - d + 4, 4)] = left.T
        for dy in (2, 1, 3, 0):
            j = lax.rem(y + dy, 4)
            op[j, rows, :] = jnp.dot(left, wd4[j], preferred_element_type=F32).astype(BF)
            if dy:
                out_ids[d, dy] = links.send(op.at[j, rows], ro.at[dy - 1, rows], device(x, y + dy, z, c))

    so[...] = jnp.zeros_like(so)
    back = {}

    def give(d):
        gx = lax.rem(x - d + 4, 4)
        rows = chunk(gx)
        for dy in (1, 3, 2):
            links.arrived(out_ids[d, dy], ro.at[dy - 1, rows])
        total = op[y, rows, :].astype(F32)
        for dy in (1, 2, 3):
            total += ro[dy - 1, rows, :].astype(F32)
        so[0:1, :] += jnp.sum(total * rg[rows, :].astype(F32), axis=0, keepdims=True)
        eo[rows, :] = (total * down_scale).astype(BF)
        for j in range(4):
            r = gx * 4 + lax.rem(inner + j, 4)
            if d == 0 and j == 0:
                ret[me] = eo[block(r), :]
            else:
                back[d, j] = links.send(eo.at[block(r)], ret.at[me], (dp, r))

    sc[...] = jnp.zeros_like(sc)
    gi_ids = {}

    def gradient(g):
        rows = rows_of(g)
        for d in (1, 2, 3):
            links.arrived(zr[g, d], rz.at[d - 1, rows])
        total = part[zh, rows, :].astype(F32)
        for d in (1, 2, 3):
            total += rz[d - 1, rows, :].astype(F32)
        gate_pre, up_pre = pre[rows, 0:128], pre[rows, 128:256]
        gate_act, up_act = gate_pre * gate_scale, up_pre * up_scale
        sig = jax.nn.sigmoid(gate_act)
        gate_grad = total * up_act * sig * (1.0 + gate_act * (1.0 - sig))
        up_grad = total * (gate_act * sig)
        sc[0:1, :] += jnp.sum(gate_grad * gate_pre, axis=0, keepdims=True)
        sc[1:2, :] += jnp.sum(up_grad * up_pre, axis=0, keepdims=True)
        gi[rows, 0:128] = (gate_grad * gate_scale).astype(BF)
        gi[rows, 128:256] = (up_grad * up_scale).astype(BF)

    def trade_gi(g):
        gi_ids[g] = links.send(gi.at[rows_of(g)], gi_far.at[rows_of(g)], far)

    for load in loads:
        load.wait()
    y_fwd(0)
    group(0)
    x_first(0)
    y_fwd(1)
    terms(0)
    y_fwd(3)
    x_second(0)
    terms(1)
    hid_fwd(0)
    y_fwd(2)
    x_first(1)
    terms(3)
    terms(2)
    project(0)
    x_second(1)
    x_far(0)
    group(1)
    group(3)
    gradient(0)
    gradient(1)
    gradient(3)
    x_far(1)
    for g in (0, 1, 3):
        trade_gi(g)
    hid_fwd(1)
    hid_fwd(3)
    group(2)
    project(1)
    project(3)
    hid_fwd(2)
    gradient(2)
    trade_gi(2)
    project(2)

    gd_ids = {}
    for d in (2, 1, 3, 0):
        j = lax.rem(y + d, 4)
        acc = jnp.dot(hz_t[0], di4[j, 0:CROWS, :], preferred_element_type=F32)
        for i in range(1, 4):
            acc += jnp.dot(hz_t[i], di4[j, i * CROWS:(i + 1) * CROWS, :], preferred_element_type=F32)
        gd[j] = acc.astype(BF)
        gd_ids["far", d] = links.send(gd.at[j], far_gd.at[quarter(y)], device(x + 2, y + d, z, c))
        if d:
            gd_ids["own", d] = links.send(gd.at[j], own_gd.at[quarter(y)], device(x, y + d, z, c))
        else:
            own_gd[quarter(y), :] = gd[j]
    give(0)
    give(1)
    sc_id = links.send(sc, sc_far, far)
    give(3)
    give(2)
    so_id = links.send(so, so_far, far)

    for g in ORDER:
        links.arrived(gi_ids[g], gi_far.at[rows_of((g + 2) % 4)])
    trade = jnp.sum(jnp.where(lax.broadcasted_iota(jnp.int32, (1, BLK), 1) == me, swapped[...], 0), axis=1, keepdims=True) > 0
    cw_sel = jnp.where(trade, cw_par[...], cw_own[...])
    cw_par[...] = cw_sel
    pos[...] = jnp.dot((cw_sel > 0).astype(BF), before, preferred_element_type=F32)

    def expand(r, _):
        hit = (pos[pl.ds(r, 1), :] == spots) & (cw_par[pl.ds(r, 1), :] > 0)
        chosen = jnp.where(trade, gi_far[block(r), :].astype(F32), gi[block(r), :].astype(F32)).astype(BF)
        spread_t[:, columns(r)] = lax.dot_general(
            chosen, jnp.where(hit, 1.0, 0.0).astype(BF), TN, preferred_element_type=F32
        ).astype(BF)
        return 0

    lax.fori_loop(0, BLK, expand, 0)

    def weight_grad(k, _):
        at = pl.ds(pl.multiple_of(k * 512, 512), 512)
        right = toks[:, :, at].reshape(BLK * TOK, 512)
        grad = jnp.dot(spread_t[...], right, preferred_element_type=F32).astype(BF).T
        grad_gate[at, :] = grad[:, 0:128]
        grad_up[at, :] = grad[:, 128:256]
        return 0

    lax.fori_loop(0, D // 512, weight_grad, 0)

    for (d, j), k in back.items():
        links.arrived(k, ret.at[lax.rem(x + d, 4) * 4 + lax.rem(inner + 4 - j, 4)])
    places = jnp.dot((comb[...] > 0).astype(BF), before, preferred_element_type=F32)
    total = jnp.zeros((TOK, 256), F32)
    for e in range(BLK):
        hit = (places[e:e + 1, :] == spots) & (comb[e:e + 1, :] > 0)
        total += (
            lax.dot_general(jnp.where(hit, 1.0, 0.0).astype(BF), ret[e], TN, preferred_element_type=F32)
            * comb_t[:, e:e + 1]
        )
    mixed[...] = total.astype(BF)
    links.arrived(sc_id, sc_far)
    links.arrived(so_id, so_far)
    for d in (1, 2, 3, 0):
        rows = quarter(lax.rem(y - d + 4, 4))
        links.arrived(gd_ids["far", d], far_gd.at[rows])
        if d:
            links.arrived(gd_ids["own", d], own_gd.at[rows])
    grad_down[...] = jnp.where(trade, far_gd[...], own_gd[...])
    grad_in[...] = jnp.where(trade, sc_far[0:2], sc[0:2]).astype(BF)
    grad_out[...] = jnp.where(trade, so_far[0:1], so[0:1]).astype(BF)
    links.finish()


def layer(*args):
    n = 160
    vm = pl.BlockSpec(memory_space=pltpu.VMEM)
    hbm = pl.BlockSpec(memory_space=pl.ANY)
    return pl.pallas_call(
        layer_kernel,
        out_shape=(
            jax.ShapeDtypeStruct((TOK, 256), BF),
            jax.ShapeDtypeStruct((D, 128), BF),
            jax.ShapeDtypeStruct((D, 128), BF),
            jax.ShapeDtypeStruct((2048, 256), BF),
            jax.ShapeDtypeStruct((2, 128), BF),
            jax.ShapeDtypeStruct((1, 256), BF),
        ),
        in_specs=[vm, vm, vm, hbm, hbm, hbm, vm, vm, vm, vm, vm],
        out_specs=[vm] * 6,
        scratch_shapes=[
            pltpu.VMEM((BLK, TOK), F32),
            pltpu.VMEM((TOK, TOK), F32),
            pltpu.VMEM((2048, 256), BF),
            pltpu.VMEM((2048, 256), BF),
            pltpu.VMEM((8, 128), F32),
            pltpu.VMEM((8, 128), F32),
            pltpu.VMEM((8, 256), F32),
            pltpu.VMEM((8, 256), F32),
            pltpu.VMEM((BLK, TOK, D), BF),
            pltpu.VMEM((D, 256), BF),
            pltpu.VMEM((BLK, TOK, 256), BF),
            pltpu.VMEM((BLK, BLK, TOK), F32),
            pltpu.VMEM((BLK, TOK), F32),
            pltpu.VMEM((BLK, TOK), F32),
            pltpu.VMEM((BLK, TOK), F32),
            pltpu.VMEM((ROWS, 256), BF),
            pltpu.VMEM((4, ROWS, 256), BF),
            pltpu.VMEM((4, 512, 256), BF),
            pltpu.VMEM((4, ROWS, 128), BF),
            pltpu.VMEM((3, ROWS, 128), BF),
            pltpu.VMEM((ROWS, 256), F32),
            pltpu.VMEM((ROWS, 128), BF),
            pltpu.VMEM((ROWS, 512), BF),
            pltpu.VMEM((4, 512, CROWS), BF),
            pltpu.VMEM((4, ROWS, 256), BF),
            pltpu.VMEM((3, ROWS, 256), BF),
            pltpu.VMEM((ROWS, 256), BF),
            pltpu.VMEM((BLK, CAP, 256), BF),
            pltpu.VMEM((4, 512, 256), BF),
            pltpu.VMEM((ROWS, 256), BF),
            pltpu.VMEM((ROWS, 256), BF),
            pltpu.VMEM((256, BLK * TOK), BF),
            pltpu.SemaphoreType.DMA((n,)),
            pltpu.SemaphoreType.DMA((n,)),
            pltpu.SemaphoreType.DMA((3,)),
        ],
        name="layer",
        compiler_params=pltpu.CompilerParams(collective_id=0, has_side_effects=True, vmem_limit_bytes=VMEM_LIMIT),
    )(*args)


def hand_over_kernel(*refs):
    count = (len(refs) - 2) // 3
    given, out, held = refs[:count], refs[count:2 * count], refs[2 * count:3 * count]
    loads = [pltpu.make_async_copy(given[i], held[i], refs[-2].at[i]) for i in range(count)]
    stores = [pltpu.make_async_copy(held[i], out[i], refs[-1].at[i]) for i in range(count)]
    for load in loads:
        load.start()
    for load, store in zip(loads, stores):
        load.wait()
        store.start()
    for store in stores:
        store.wait()


def hand_over(arrays):
    hbm = pl.BlockSpec(memory_space=pl.ANY)
    return pl.pallas_call(
        hand_over_kernel,
        out_shape=[jax.ShapeDtypeStruct(a.shape, a.dtype) for a in arrays],
        in_specs=[hbm] * len(arrays),
        out_specs=[hbm] * len(arrays),
        scratch_shapes=[pltpu.VMEM(a.shape, a.dtype) for a in arrays]
        + [pltpu.SemaphoreType.DMA((len(arrays),))] * 2,
        name="hand_over",
        compiler_params=pltpu.CompilerParams(vmem_limit_bytes=VMEM_LIMIT),
    )(*arrays)


def per_device(
    tokens, cotangent, routes, router_weight, w_gate, w_up, w_down,
    scale_gate, scale_up, scale_down, swapped,
):
    mixed, grad_gate, grad_up, grad_down, grad_in, grad_out = hand_over(layer(
        routes.T, router_weight.T, cotangent, tokens, w_gate[0], w_up[0], w_down[0],
        scale_gate, scale_up, scale_down, swapped[None],
    ))
    return mixed, grad_gate[None], grad_up[None], grad_down[None], grad_in[None], grad_out


def solution(mesh):
    in_specs = (
        P("expert", None),
        P("expert", "dp"),
        P("expert", None),
        P("expert", None),
        P("expert", None, "dp"),
        P("expert", None, "dp"),
        P("expert", None, "dp"),
        P("expert", "dp"),
        P("expert", "dp"),
        P("expert", "dp"),
        P(),
    )
    out_specs = (
        P("expert", "dp"),
        P("expert", None, "dp"),
        P("expert", None, "dp"),
        P("expert", None, "dp"),
        P("expert", None, "dp"),
        P("expert", "dp"),
    )
    return jax.shard_map(
        per_device, mesh=mesh, in_specs=in_specs, out_specs=out_specs, check_vma=False
    )
```

```python
import jax
import jax.numpy as jnp
from jax import lax
from jax.experimental import pallas as pl
from jax.experimental.pallas import tpu as pltpu
from jax.sharding import PartitionSpec as P

MESH = pl.DeviceIdType.MESH
BF = jnp.bfloat16
F32 = jnp.float32
CAP = 80
BLK = 16
TOK = 128
D = 4096
ROWS = BLK * CAP
CROWS = ROWS // 4
ORDER = (0, 1, 3, 2)
VMEM_LIMIT = 60 * 2**20
NT = (((1,), (1,)), ((), ()))
TN = (((0,), (0,)), ((), ()))


def place():
    dp = lax.axis_index("dp")
    ex = lax.axis_index("expert")
    y, zh = lax.div(dp, 4), lax.rem(dp, 4)
    x, zl, c = lax.div(ex, 4), lax.rem(lax.div(ex, 2), 2), lax.rem(ex, 2)
    return x, y, zh * 2 + zl, c


def device(x, y, z, c):
    x, y, z, c = lax.rem(x + 4, 4), lax.rem(y + 4, 4), lax.rem(z + 8, 8), lax.rem(c + 2, 2)
    return (y * 4 + lax.div(z, 2), slot(x, z, c))


def slot(x, z, c):
    return lax.rem(x + 4, 4) * 4 + lax.rem(z + 8, 2) * 2 + c


class Links:
    def __init__(self, send_sems, recv_sems, other):
        self.ss, self.rs, self.other = send_sems, recv_sems, other
        self.copies = []

    def send(self, src, dst, to):
        i = len(self.copies)
        copy = pltpu.make_async_remote_copy(
            src_ref=src,
            dst_ref=dst,
            send_sem=self.ss.at[i],
            recv_sem=self.rs.at[i],
            device_id=to,
            device_id_type=MESH,
        )
        copy.start()
        self.copies.append(copy)
        return i

    def arrived(self, i, dst):
        pltpu.make_async_remote_copy(
            src_ref=dst,
            dst_ref=dst,
            send_sem=self.ss.at[i],
            recv_sem=self.rs.at[i],
            device_id=self.other,
            device_id_type=MESH,
        ).wait_recv()

    def finish(self):
        for copy in self.copies:
            copy.wait_send()


def greet(devices):
    barrier = pltpu.get_barrier_semaphore()
    for to in devices:
        pl.semaphore_signal(barrier, inc=1, device_id=to, device_id_type=MESH)
    pl.semaphore_wait(barrier, len(devices))


def layer_kernel(
    routes, weights, cot, tok, wg, wu, wd, sg, su, sd, swapped,
    mixed, grad_gate, grad_up, grad_down, grad_in, grad_out,
    comb, comb_t, own_gd, far_gd, sc, sc_far, so, so_far,
    toks, w_in, cots, combs, cw_own, cw_par, pos, rg, di4, wd4, part, rz,
    pre, hid, hz, hz_t, op, ro, eo, ret, gd, gi, gi_far, spread_t, ss, rs, local,
):
    x, y, z, c = place()
    zl = lax.rem(z, 2)
    zh = lax.div(z, 2)
    me = slot(x, z, c)
    inner = lax.rem(me, 4)
    dp = lax.axis_index("dp")
    sibling = device(x, y, z, 1 - c)
    far = device(x + 2, y, z, c)
    up, down = device(x, y, z + 1, c), device(x, y, z - 1, c)
    chip = x * 2 + zl
    links = Links(ss, rs, sibling)

    def chip_at(k):
        q = lax.rem(chip + k + 8, 8)
        return lax.div(q, 2), zh * 2 + lax.rem(q, 2)

    def columns(j):
        return pl.ds(pl.multiple_of(j * 128, 128), 128)

    def quarter(j):
        return pl.ds(pl.multiple_of(j * 512, 512), 512)

    def chunk(j):
        return pl.ds(pl.multiple_of(j * CROWS, CROWS), CROWS)

    def block(r):
        return pl.ds(pl.multiple_of(r * CAP, CAP), CAP)

    loads = [
        pltpu.make_async_copy(tok, toks.at[me], local.at[0]),
        pltpu.make_async_copy(wg, w_in.at[:, pl.ds(0, 128)], local.at[1]),
        pltpu.make_async_copy(wu, w_in.at[:, pl.ds(128, 128)], local.at[2]),
    ]
    for load in loads:
        load.start()

    names = lax.broadcasted_iota(jnp.int32, (TOK, TOK), 0)
    dense = jnp.zeros((TOK, TOK), F32)
    for k in range(routes.shape[0]):
        dense += jnp.where(routes[k:k + 1, :] == names, weights[k:k + 1, :], 0.0)
    comb[...] = dense[0:BLK]
    comb_t[...] = dense.T

    peers = [(dp, lax.rem(me + k, 16)) for k in range(1, 16)]
    peers.append(device(x, y, z - 1 + 2 * zl, c))
    for d in range(1, 4):
        peers.append(device(x, y + d, z, c))
        peers.append(device(x, y, z + 2 * d, c))
        peers.append(device(x + 2, y + d, z, c))
    greet(peers)

    first = []
    for k in range(1, 8):
        qx, qz = chip_at(k)
        to = device(qx, y, qz, c)
        first.append((k, links.send(comb, combs.at[me], to), links.send(cot, cots.at[me], to)))
    over = [(0, links.send(comb, combs.at[me], sibling), links.send(cot, cots.at[me], sibling))]
    wd_ids = []
    for d in (1, 3, 2):
        wd_ids.append((d, links.send(wd.at[quarter(lax.rem(y + d, 4))], wd4.at[y], device(x, y + d, z, c))))

    lower, upper = pl.ds(0, 64), pl.ds(64, 64)
    halves = {"l": lower, "u": upper}
    pair = {}

    def to_sibling(d, dz, rows):
        s = slot(x - d, z + dz, c)
        pair.setdefault((d, dz), []).append((links.send(toks.at[s, rows], toks.at[s, rows], sibling), rows))

    z_ids, x_ids, f_ids = {}, {}, {}
    z_ids["l"] = links.send(tok.at[lower], toks.at[me, lower], up)
    z_ids["u"] = links.send(tok.at[upper], toks.at[me, upper], down)
    for d, h in ((1, "l"), (3, "u")):
        x_ids[d, 0, h] = links.send(tok.at[halves[h]], toks.at[me, halves[h]], device(x + d, y, z, c))
    pair[0, 0] = [(links.send(tok, toks.at[me], sibling), pl.ds(0, TOK))]

    def z_own():
        s = slot(x, z + 1, c)
        for h, order in (("l", (1, 3)), ("u", (3, 1))):
            rows = halves[h]
            links.arrived(z_ids[h], toks.at[s, rows])
            for d in order:
                x_ids[d, 1, h] = links.send(toks.at[s, rows], toks.at[s, rows], device(x + d, y, z, c))
            to_sibling(0, 1, rows)

    def x_first(dz):
        for d, h in ((1, "l"), (3, "u")):
            s = slot(x - d, z + dz, c)
            rows = halves[h]
            links.arrived(x_ids[d, dz, h], toks.at[s, rows])
            f_ids[d, dz] = links.send(toks.at[s, rows], toks.at[s, rows], device(x + d, y, z, c))
            to_sibling(d, dz, rows)

    def x_second(dz):
        for d, h in ((1, "u"), (3, "l")):
            s = slot(x - d, z + dz, c)
            links.arrived(x_ids[d, dz, h], toks.at[s, halves[h]])
            to_sibling(d, dz, halves[h])

    def x_far(dz):
        for d, h in ((1, "l"), (3, "u")):
            s = slot(x + 2, z + dz, c)
            links.arrived(f_ids[d, dz], toks.at[s, halves[h]])
            to_sibling(2, dz, halves[h])

    combs[me] = comb[...]
    cots[me] = cot[...]
    wd4[y] = wd[quarter(y), :]
    for k, ia, ib in first:
        qx, qz = chip_at(-k)
        s = slot(qx, qz, c)
        links.arrived(ia, combs.at[s])
        links.arrived(ib, cots.at[s])
        over.append((k, links.send(combs.at[s], combs.at[s], sibling), links.send(cots.at[s], cots.at[s], sibling)))
    for d, h in ((1, "u"), (3, "l")):
        x_ids[d, 0, h] = links.send(tok.at[halves[h]], toks.at[me, halves[h]], device(x + d, y, z, c))
    z_own()
    for k, ia, ib in over:
        qx, qz = chip_at(-k)
        s = slot(qx, qz, 1 - c)
        links.arrived(ia, combs.at[s])
        links.arrived(ib, cots.at[s])

    experts = lax.broadcasted_iota(jnp.int32, (BLK, BLK, TOK), 1)
    table = combs[...]
    cw = jnp.sum(jnp.where(experts == me, table, 0.0), axis=1)
    cw_own[...] = cw
    cw_par[...] = jnp.sum(jnp.where(experts == lax.rem(me + 8, 16), table, 0.0), axis=1)
    before = (
        lax.broadcasted_iota(jnp.int32, (TOK, TOK), 0) < lax.broadcasted_iota(jnp.int32, (TOK, TOK), 1)
    ).astype(F32).astype(BF)
    pos[...] = jnp.dot((cw > 0).astype(BF), before, preferred_element_type=F32)
    spots = lax.broadcasted_iota(jnp.int32, (CAP, TOK), 0).astype(F32)
    down_scale = sd[...].astype(F32)

    def compact(r, _):
        weight = cw_own[pl.ds(r, 1), :]
        hit = (pos[pl.ds(r, 1), :] == spots) & (weight > 0)
        picked = jnp.dot(jnp.where(hit, 1.0, 0.0).astype(BF), cots[r], preferred_element_type=F32)
        w = jnp.sum(jnp.where(hit, weight, 0.0), axis=1, keepdims=True)
        routed = (picked * w).astype(BF)
        rg[block(r), :] = routed
        di4[y, block(r), :] = (routed.astype(F32) * down_scale).astype(BF)
        return 0

    def rows_of(d, part=None):
        start = lax.rem(x - d + 4, 4) * CROWS
        if part is None:
            return pl.ds(pl.multiple_of(start, CROWS), CROWS)
        return pl.ds(pl.multiple_of(start + part * (CROWS // 2), CROWS // 2), CROWS // 2)

    y_ids = {}
    for g in ORDER:
        at = lax.rem(x - g + 4, 4) * 4
        lax.fori_loop(at, at + 4, compact, 0)
        rows = rows_of(g)
        for d in (1, 3):
            y_ids[g, d] = links.send(di4.at[y, rows], di4.at[y, rows], device(x, y + d, z, c))
    for d, i in wd_ids:
        links.arrived(i, wd4.at[lax.rem(y - d + 4, 4)])

    def y_fwd(g):
        for d, h in ((1, 0), (3, 1)):
            j = lax.rem(y - d + 4, 4)
            links.arrived(y_ids[g, d], di4.at[j, rows_of(g)])
            rows = rows_of(g, h)
            y_ids[g, d, "f"] = links.send(di4.at[j, rows], di4.at[j, rows], device(x, y + d, z, c))

    zr = {}

    def terms(g):
        rows = rows_of(g)
        for d, h in ((1, 0), (3, 1)):
            links.arrived(y_ids[g, d, "f"], di4.at[lax.rem(y + 2, 4), rows_of(g, h)])
        acc = lax.dot_general(di4[0, rows, :], wd4[0], NT, preferred_element_type=F32)
        for j in range(1, 4):
            acc += lax.dot_general(di4[j, rows, :], wd4[j], NT, preferred_element_type=F32)
        acc = acc.astype(BF)
        for j in range(4):
            part[j, rows, :] = acc[:, j * 128:(j + 1) * 128]
        for d in (2, 1, 3):
            zr[g, d] = links.send(part.at[lax.rem(zh + d, 4), rows], rz.at[d - 1, rows], device(x, y, z + 2 * d, c))

    gate_scale = sg[...].astype(F32)
    up_scale = su[...].astype(F32)
    hid_ids = {}

    def group(d):
        gx = lax.rem(x - d + 4, 4)
        for dz in (0, 1):
            s = slot(x - d, z + dz, 1 - c)
            for i, rows in pair[d, dz]:
                links.arrived(i, toks.at[s, rows])

        def deepen(k, acc):
            at = pl.ds(pl.multiple_of(k * 1024, 1024), 1024)
            left = toks[pl.ds(gx * 4, 4), :, at].reshape(4 * TOK, 1024)
            return acc + jnp.dot(left, w_in[at, :], preferred_element_type=F32)

        acc = lax.fori_loop(0, 4, deepen, jnp.zeros((4 * TOK, 256), F32))
        for j in range(4):
            r = gx * 4 + j
            hit = (pos[pl.ds(r, 1), :] == spots) & (cw_own[pl.ds(r, 1), :] > 0)
            pre[block(r), :] = jnp.dot(
                jnp.where(hit, 1.0, 0.0), acc[j * TOK:(j + 1) * TOK], precision=lax.Precision.HIGHEST,
                preferred_element_type=F32,
            )
        rows = chunk(gx)
        gate_act = pre[rows, 0:128] * gate_scale
        up_act = pre[rows, 128:256] * up_scale
        hid[rows, :] = (gate_act * jax.nn.sigmoid(gate_act) * up_act).astype(BF)
        hz[rows, columns(zh)] = hid[rows, :]
        for dz in (1, 3):
            hid_ids[d, dz] = links.send(hid.at[rows], hz.at[rows, columns(zh)], device(x, y, z + 2 * dz, c))

    def hid_fwd(d):
        for dz, h in ((1, 0), (3, 1)):
            at = columns(lax.rem(zh - dz + 4, 4))
            links.arrived(hid_ids[d, dz], hz.at[rows_of(d), at])
            rows = rows_of(d, h)
            hid_ids[d, dz, "f"] = links.send(hz.at[rows, at], hz.at[rows, at], device(x, y, z + 2 * dz, c))

    out_ids = {}

    def project(d):
        rows = chunk(lax.rem(x - d + 4, 4))
        for dz, h in ((1, 0), (3, 1)):
            links.arrived(hid_ids[d, dz, "f"], hz.at[rows_of(d, h), columns(lax.rem(zh + 2, 4))])
        left = hz[rows, :]
        hz_t[lax.rem(x - d + 4, 4)] = left.T
        for dy in (2, 1, 3, 0):
            j = lax.rem(y + dy, 4)
            op[j, rows, :] = jnp.dot(left, wd4[j], preferred_element_type=F32).astype(BF)
            if dy:
                out_ids[d, dy] = links.send(op.at[j, rows], ro.at[dy - 1, rows], device(x, y + dy, z, c))

    so[...] = jnp.zeros_like(so)
    back = {}

    def give(d):
        gx = lax.rem(x - d + 4, 4)
        rows = chunk(gx)
        for dy in (1, 3, 2):
            links.arrived(out_ids[d, dy], ro.at[dy - 1, rows])
        total = op[y, rows, :].astype(F32)
        for dy in (1, 2, 3):
            total += ro[dy - 1, rows, :].astype(F32)
        so[0:1, :] += jnp.sum(total * rg[rows, :].astype(F32), axis=0, keepdims=True)
        eo[rows, :] = (total * down_scale).astype(BF)
        for j in range(4):
            r = gx * 4 + lax.rem(inner + j, 4)
            if d == 0 and j == 0:
                ret[me] = eo[block(r), :]
            else:
                back[d, j] = links.send(eo.at[block(r)], ret.at[me], (dp, r))

    sc[...] = jnp.zeros_like(sc)
    gi_ids = {}

    def gradient(g):
        rows = rows_of(g)
        for d in (1, 2, 3):
            links.arrived(zr[g, d], rz.at[d - 1, rows])
        total = part[zh, rows, :].astype(F32)
        for d in (1, 2, 3):
            total += rz[d - 1, rows, :].astype(F32)
        gate_pre, up_pre = pre[rows, 0:128], pre[rows, 128:256]
        gate_act, up_act = gate_pre * gate_scale, up_pre * up_scale
        sig = jax.nn.sigmoid(gate_act)
        gate_grad = total * up_act * sig * (1.0 + gate_act * (1.0 - sig))
        up_grad = total * (gate_act * sig)
        sc[0:1, :] += jnp.sum(gate_grad * gate_pre, axis=0, keepdims=True)
        sc[1:2, :] += jnp.sum(up_grad * up_pre, axis=0, keepdims=True)
        gi[rows, 0:128] = (gate_grad * gate_scale).astype(BF)
        gi[rows, 128:256] = (up_grad * up_scale).astype(BF)

    def trade_gi(g):
        gi_ids[g] = links.send(gi.at[rows_of(g)], gi_far.at[rows_of(g)], far)

    for load in loads:
        load.wait()
    y_fwd(0)
    group(0)
    x_first(0)
    y_fwd(1)
    terms(0)
    y_fwd(3)
    x_second(0)
    terms(1)
    hid_fwd(0)
    y_fwd(2)
    x_first(1)
    terms(3)
    terms(2)
    project(0)
    x_second(1)
    x_far(0)
    group(1)
    group(3)
    gradient(0)
    gradient(1)
    gradient(3)
    x_far(1)
    for g in (0, 1, 3):
        trade_gi(g)
    hid_fwd(1)
    hid_fwd(3)
    group(2)
    project(1)
    project(3)
    hid_fwd(2)
    gradient(2)
    trade_gi(2)
    project(2)

    gd_ids = {}
    for d in (2, 1, 3, 0):
        j = lax.rem(y + d, 4)
        acc = jnp.dot(hz_t[0], di4[j, 0:CROWS, :], preferred_element_type=F32)
        for i in range(1, 4):
            acc += jnp.dot(hz_t[i], di4[j, i * CROWS:(i + 1) * CROWS, :], preferred_element_type=F32)
        gd[j] = acc.astype(BF)
        gd_ids["far", d] = links.send(gd.at[j], far_gd.at[quarter(y)], device(x + 2, y + d, z, c))
        if d:
            gd_ids["own", d] = links.send(gd.at[j], own_gd.at[quarter(y)], device(x, y + d, z, c))
        else:
            own_gd[quarter(y), :] = gd[j]
    give(0)
    give(1)
    sc_id = links.send(sc, sc_far, far)
    give(3)
    give(2)
    so_id = links.send(so, so_far, far)

    for g in ORDER:
        links.arrived(gi_ids[g], gi_far.at[rows_of((g + 2) % 4)])
    trade = jnp.sum(jnp.where(lax.broadcasted_iota(jnp.int32, (1, BLK), 1) == me, swapped[...], 0), axis=1, keepdims=True) > 0
    cw_sel = jnp.where(trade, cw_par[...], cw_own[...])
    cw_par[...] = cw_sel
    pos[...] = jnp.dot((cw_sel > 0).astype(BF), before, preferred_element_type=F32)

    def expand(r, _):
        hit = (pos[pl.ds(r, 1), :] == spots) & (cw_par[pl.ds(r, 1), :] > 0)
        chosen = jnp.where(trade, gi_far[block(r), :].astype(F32), gi[block(r), :].astype(F32)).astype(BF)
        spread_t[:, columns(r)] = lax.dot_general(
            chosen, jnp.where(hit, 1.0, 0.0).astype(BF), TN, preferred_element_type=F32
        ).astype(BF)
        return 0

    lax.fori_loop(0, BLK, expand, 0)

    def weight_grad(k, _):
        at = pl.ds(pl.multiple_of(k * 512, 512), 512)
        right = toks[:, :, at].reshape(BLK * TOK, 512)
        grad = jnp.dot(spread_t[...], right, preferred_element_type=F32).astype(BF).T
        grad_gate[at, :] = grad[:, 0:128]
        grad_up[at, :] = grad[:, 128:256]
        return 0

    lax.fori_loop(0, D // 512, weight_grad, 0)

    for (d, j), k in back.items():
        links.arrived(k, ret.at[lax.rem(x + d, 4) * 4 + lax.rem(inner + 4 - j, 4)])
    places = jnp.dot((comb[...] > 0).astype(BF), before, preferred_element_type=F32)
    total = jnp.zeros((TOK, 256), F32)
    for e in range(BLK):
        hit = (places[e:e + 1, :] == spots) & (comb[e:e + 1, :] > 0)
        total += (
            lax.dot_general(jnp.where(hit, 1.0, 0.0).astype(BF), ret[e], TN, preferred_element_type=F32)
            * comb_t[:, e:e + 1]
        )
    mixed[...] = total.astype(BF)
    links.arrived(sc_id, sc_far)
    links.arrived(so_id, so_far)
    for d in (1, 2, 3, 0):
        rows = quarter(lax.rem(y - d + 4, 4))
        links.arrived(gd_ids["far", d], far_gd.at[rows])
        if d:
            links.arrived(gd_ids["own", d], own_gd.at[rows])
    grad_down[...] = jnp.where(trade, far_gd[...], own_gd[...])
    grad_in[...] = jnp.where(trade, sc_far[0:2], sc[0:2]).astype(BF)
    grad_out[...] = jnp.where(trade, so_far[0:1], so[0:1]).astype(BF)
    links.finish()


def layer(*args):
    n = 160
    vm = pl.BlockSpec(memory_space=pltpu.VMEM)
    hbm = pl.BlockSpec(memory_space=pl.ANY)
    return pl.pallas_call(
        layer_kernel,
        out_shape=(
            jax.ShapeDtypeStruct((TOK, 256), BF),
            jax.ShapeDtypeStruct((D, 128), BF),
            jax.ShapeDtypeStruct((D, 128), BF),
            jax.ShapeDtypeStruct((2048, 256), BF),
            jax.ShapeDtypeStruct((2, 128), BF),
            jax.ShapeDtypeStruct((1, 256), BF),
        ),
        in_specs=[vm, vm, vm, hbm, hbm, hbm, vm, vm, vm, vm, vm],
        out_specs=[vm] * 6,
        scratch_shapes=[
            pltpu.VMEM((BLK, TOK), F32),
            pltpu.VMEM((TOK, TOK), F32),
            pltpu.VMEM((2048, 256), BF),
            pltpu.VMEM((2048, 256), BF),
            pltpu.VMEM((8, 128), F32),
            pltpu.VMEM((8, 128), F32),
            pltpu.VMEM((8, 256), F32),
            pltpu.VMEM((8, 256), F32),
            pltpu.VMEM((BLK, TOK, D), BF),
            pltpu.VMEM((D, 256), BF),
            pltpu.VMEM((BLK, TOK, 256), BF),
            pltpu.VMEM((BLK, BLK, TOK), F32),
            pltpu.VMEM((BLK, TOK), F32),
            pltpu.VMEM((BLK, TOK), F32),
            pltpu.VMEM((BLK, TOK), F32),
            pltpu.VMEM((ROWS, 256), BF),
            pltpu.VMEM((4, ROWS, 256), BF),
            pltpu.VMEM((4, 512, 256), BF),
            pltpu.VMEM((4, ROWS, 128), BF),
            pltpu.VMEM((3, ROWS, 128), BF),
            pltpu.VMEM((ROWS, 256), F32),
            pltpu.VMEM((ROWS, 128), BF),
            pltpu.VMEM((ROWS, 512), BF),
            pltpu.VMEM((4, 512, CROWS), BF),
            pltpu.VMEM((4, ROWS, 256), BF),
            pltpu.VMEM((3, ROWS, 256), BF),
            pltpu.VMEM((ROWS, 256), BF),
            pltpu.VMEM((BLK, CAP, 256), BF),
            pltpu.VMEM((4, 512, 256), BF),
            pltpu.VMEM((ROWS, 256), BF),
            pltpu.VMEM((ROWS, 256), BF),
            pltpu.VMEM((256, BLK * TOK), BF),
            pltpu.SemaphoreType.DMA((n,)),
            pltpu.SemaphoreType.DMA((n,)),
            pltpu.SemaphoreType.DMA((3,)),
        ],
        name="layer",
        compiler_params=pltpu.CompilerParams(collective_id=0, has_side_effects=True, vmem_limit_bytes=VMEM_LIMIT),
    )(*args)


def hand_over_kernel(*refs):
    count = (len(refs) - 2) // 3
    given, out, held = refs[:count], refs[count:2 * count], refs[2 * count:3 * count]
    parts = []
    for i in range(count):
        rows = given[i].shape[0]
        cut = rows // 4 if rows >= 2048 else rows
        parts += [(i, pl.ds(at, cut)) for at in range(0, rows, cut)]
    loads = [pltpu.make_async_copy(given[i].at[r], held[i].at[r], refs[-2].at[n]) for n, (i, r) in enumerate(parts)]
    stores = [pltpu.make_async_copy(held[i].at[r], out[i].at[r], refs[-1].at[n]) for n, (i, r) in enumerate(parts)]
    for load in loads:
        load.start()
    for load, store in zip(loads, stores):
        load.wait()
        store.start()
    for store in stores:
        store.wait()


def hand_over(arrays):
    hbm = pl.BlockSpec(memory_space=pl.ANY)
    return pl.pallas_call(
        hand_over_kernel,
        out_shape=[jax.ShapeDtypeStruct(a.shape, a.dtype) for a in arrays],
        in_specs=[hbm] * len(arrays),
        out_specs=[hbm] * len(arrays),
        scratch_shapes=[pltpu.VMEM(a.shape, a.dtype) for a in arrays]
        + [pltpu.SemaphoreType.DMA((4 * len(arrays),))] * 2,
        name="hand_over",
        compiler_params=pltpu.CompilerParams(vmem_limit_bytes=VMEM_LIMIT),
    )(*arrays)


def per_device(
    tokens, cotangent, routes, router_weight, w_gate, w_up, w_down,
    scale_gate, scale_up, scale_down, swapped,
):
    mixed, grad_gate, grad_up, grad_down, grad_in, grad_out = hand_over(layer(
        routes.T, router_weight.T, cotangent, tokens, w_gate[0], w_up[0], w_down[0],
        scale_gate, scale_up, scale_down, swapped[None],
    ))
    return mixed, grad_gate[None], grad_up[None], grad_down[None], grad_in[None], grad_out


def solution(mesh):
    in_specs = (
        P("expert", None),
        P("expert", "dp"),
        P("expert", None),
        P("expert", None),
        P("expert", None, "dp"),
        P("expert", None, "dp"),
        P("expert", None, "dp"),
        P("expert", "dp"),
        P("expert", "dp"),
        P("expert", "dp"),
        P(),
    )
    out_specs = (
        P("expert", "dp"),
        P("expert", None, "dp"),
        P("expert", None, "dp"),
        P("expert", None, "dp"),
        P("expert", None, "dp"),
        P("expert", "dp"),
    )
    return jax.shard_map(
        per_device, mesh=mesh, in_specs=in_specs, out_specs=out_specs, check_vma=False
    )
```
